512 devices in a mesh: row: 16 (over z), col: 8 (over x, y_lo), rep: 4 (over y_hi, core).
Axes of the slice: x: 4, y: 4 (y_hi: 2, y_lo: 2; y = y_hi * 2 + y_lo), z: 16, core: 2. Of those that a mesh axis runs over, the one named last changes fastest.
Arguments:
- density: bfloat16 [8192, 8192], P(('row', 'rep'), 'col'), as said below
- reach: int32 [64], replicated, may hold values from 8 to 32
- slab_start: int32 [1], replicated, may hold values from 0 to 4096
Outputs:
- purified: float32 [4096, 8192], P('row', ('col', 'rep'))
The draws below stay inside these ranges and needn't reach their ends.
Inputs may be any that keep to these rules, and one draw needn't show every extreme that they name: density is exactly symmetric.
All inputs are finite; a program needn't handle non-finite values.
Results may differ from the reference program's by a relative error of at most 0.0018.
Values may be sent and summed in bfloat16 or wider, within the bound.
A program may use at most 64 MiB of HBM per device.

```python
import math
import jax
import jax.numpy as jnp
from jax import lax

BLK = 128
NBLK = 64
ORDER = 8192
SLAB = 4096


def draw_density(key, part):
    first = jax.random.fold_in(jax.random.fold_in(key, 11), 0)
    raw = jax.random.normal(first, (ORDER, ORDER), jnp.float32)
    factor = 0.7071068 * 3.7 / math.sqrt(ORDER)
    return ((raw + raw.T) * factor).astype(jnp.bfloat16)


def with_ends(array, rng, least, high):
    longest = array.shape.index(max(array.shape))
    spots = []
    for shift in (0, 1):
        where = [jax.random.randint(jax.random.fold_in(rng, axis), (), 0, length) for axis, length in enumerate(array.shape)]
        where[longest] = (where[longest] + shift) % array.shape[longest]
        spots.append(tuple(where))
    return array.at[spots[0]].set(least).at[spots[1]].set(high)


def setup_inputs(seed: int = 0) -> dict:
    keys = jax.random.split(jax.random.key(seed), 4)
    return {
        "density": draw_density(jax.random.fold_in(keys[3], 71), 0),
        "reach": with_ends(jax.random.randint(keys[1], (NBLK,), NBLK // 8, NBLK // 2 + 1), jax.random.fold_in(keys[1], 1), NBLK // 8, (NBLK // 2 + 1) - 1).astype(jnp.int32),
        "slab_start": jax.random.randint(keys[2], (1,), 0, ORDER - SLAB + 1).astype(jnp.int32),
    }


def block_pattern(reach):
    blocks = jnp.arange(NBLK)
    spread = jnp.abs(blocks[:, None] - blocks[None, :])
    spread = jnp.minimum(spread, NBLK - spread)
    return spread <= jnp.minimum(reach[:, None], reach[None, :])


def reference(density, reach, slab_start):
    pattern = block_pattern(reach)
    entries = jnp.repeat(jnp.repeat(pattern, BLK, axis=0), BLK, axis=1)
    masked = jnp.where(entries, density, jnp.zeros_like(density))
    slab_rows = lax.dynamic_slice_in_dim(masked, slab_start[0], SLAB, 0)
    square = jnp.dot(slab_rows, masked, preferred_element_type=jnp.float32)
    square_low = square.astype(jnp.bfloat16)
    cube = jnp.dot(square_low, masked, preferred_element_type=jnp.float32)
    return 3.0 * square - 2.0 * cube
```

```python
import jax
import jax.numpy as jnp
from jax import lax
from jax.experimental import pallas as pl
from jax.experimental.pallas import tpu as pltpu
from jax.sharding import PartitionSpec as P

BLOCK = 128
PANEL = 256
WIDE = 512
PLANES = 16
CHIPS = 16
SIDE = 4
BLOCKS = 64
MESH = pl.DeviceIdType.MESH
F32 = jnp.float32
BF16 = jnp.bfloat16


def rem(value, count):
    return lax.rem(value + count, count)


def half_piece(chip, half):
    return (chip, pl.ds(half * 128, 128))


def quarter_piece(chip, half, quarter):
    return (chip, pl.ds(half * 128 + quarter * 64, 64))


def kernel(
    density_ref, reach_ref, start_ref, out_ref,
    staged, panel, slab, square_low, extract, extract_in, part, part_in, cube_in, square,
    swap_send, swap_recv, ring_send, ring_recv, pair_send, pair_recv, plane_send, plane_recv,
):
    z = lax.axis_index("row")
    col = lax.axis_index("col")
    rep = lax.axis_index("rep")
    x, y_low = lax.div(col, 2), lax.rem(col, 2)
    y_high, core = lax.div(rep, 2), lax.rem(rep, 2)
    y = y_high * 2 + y_low
    other = 1 - core

    def chip_device(x_to, y_to):
        return (z, x_to * 2 + lax.rem(y_to, 2), lax.div(y_to, 2) * 2 + core)

    def chip_index(x_to, y_to):
        return x_to * 4 + lax.rem(y_to, 2) * 2 + lax.div(y_to, 2)

    def step(axis, offset):
        if axis == 0:
            return rem(x + offset, SIDE), y
        return x, rem(y + offset, SIDE)

    def place(first, first_offset, second_offset):
        if first == 0:
            return chip_index(rem(x + first_offset, SIDE), rem(y + second_offset, SIDE))
        return chip_index(rem(x + second_offset, SIDE), rem(y + first_offset, SIDE))

    up = (rem(z + 1, PLANES), col, rep)
    down = (rem(z - 1, PLANES), col, rep)
    sibling = (z, col, y_high * 2 + other)
    chip = chip_index(x, y)

    barrier = pltpu.get_barrier_semaphore()
    partners = [up, down]
    for axis in (0, 1):
        for offset in (1, -1):
            partners.append(chip_device(*step(axis, offset)))
    for offset in (1, 2, 3):
        partners.append((z, col, rem(rep + offset, 4)))
    for partner in partners:
        pl.semaphore_signal(barrier, inc=1, device_id=partner, device_id_type=MESH)

    own_block = z * 4 + rep
    own_reach = reach_ref[own_block]
    for block in range(8):
        column_block = col * 8 + block
        spread = lax.abs(column_block - own_block)
        spread = lax.min(spread, BLOCKS - spread)
        kept = spread <= lax.min(reach_ref[column_block], own_reach)
        scale = jnp.where(kept, 1.0, 0.0).astype(F32)
        values = density_ref[:, block * BLOCK:(block + 1) * BLOCK].astype(F32) * scale
        place_at = pl.ds((block % 4) * BLOCK, BLOCK)
        staged[block // 4, :, place_at] = values.astype(BF16)
    pl.semaphore_wait(barrier, len(partners))

    stays = y_high == core

    def swap_copy(side, sender):
        return pltpu.make_async_remote_copy(
            src_ref=staged.at[side],
            dst_ref=panel.at[z, pl.ds(sender * BLOCK, BLOCK)],
            send_sem=swap_send.at[side],
            recv_sem=swap_recv.at[sender],
            device_id=(z, col, side * 2 + y_high),
            device_id_type=MESH,
        )

    for side in (0, 1):
        is_own = jnp.logical_and(stays, y_high == side)

        @pl.when(jnp.logical_not(is_own))
        def _():
            swap_copy(side, core).start()

        @pl.when(is_own)
        def _():
            panel[z, pl.ds(side * BLOCK, BLOCK), :] = staged[side]

    for sender in (0, 1):
        is_own = jnp.logical_and(stays, core == sender)

        @pl.when(jnp.logical_not(is_own))
        def _():
            swap_copy(sender, sender).wait_recv()

    def ring_copy(way, distance, part_index):
        behind = distance - 1
        slot = rem(z - behind, PLANES) if way == 0 else rem(z + behind, PLANES)
        return pltpu.make_async_remote_copy(
            src_ref=panel.at[slot, pl.ds(part_index * 128, 128)],
            dst_ref=panel.at[slot, pl.ds(part_index * 128, 128)],
            send_sem=ring_send.at[way, behind, part_index],
            recv_sem=ring_recv.at[way, behind, part_index],
            device_id=up if way == 0 else down,
            device_id_type=MESH,
        )

    both = [(way, part_index) for part_index in (0, 1) for way in (0, 1)]
    last = [(0, 0), (1, 1)]
    for way, part_index in both:
        ring_copy(way, 1, part_index).start()

    def ring_step(distance, carry):
        for way, part_index in both:
            ring_copy(way, distance - 1, part_index).wait_recv()
            ring_copy(way, distance, part_index).start()
        return carry

    lax.fori_loop(2, 8, ring_step, 0)
    for way, part_index in last:
        ring_copy(way, 7, part_index).wait_recv()
        ring_copy(way, 8, part_index).start()
    for way, part_index in both:
        if (way, part_index) not in last:
            ring_copy(way, 7, part_index).wait_recv()
    for way, part_index in last:
        ring_copy(way, 8, part_index).wait_recv()

    first_row = start_ref[0] + z * PANEL
    first_block = lax.div(first_row, PANEL)
    inside = lax.rem(first_row, PANEL)
    mine = lax.rem(first_block, 2) == core
    held = jnp.where(mine, lax.div(first_block, 2), lax.min(lax.div(first_block + 1, 2), PLANES - 1))
    shift = jnp.where(mine, inside, inside - PANEL)
    rows = lax.broadcasted_iota(jnp.int32, (PANEL, PANEL), 0)
    columns = lax.broadcasted_iota(jnp.int32, (PANEL, PANEL), 1)
    pick = jnp.where(columns == rows + shift, 1.0, 0.0).astype(BF16)
    for side in (0, 1):
        block = panel[held, :, side * PANEL:(side + 1) * PANEL]
        extract[side] = jnp.dot(pick, block, preferred_element_type=F32).astype(BF16)

    def pair_copy(index, source, target):
        return pltpu.make_async_remote_copy(
            src_ref=source.at[other],
            dst_ref=target,
            send_sem=pair_send.at[index],
            recv_sem=pair_recv.at[index],
            device_id=sibling,
            device_id_type=MESH,
        )

    extract_copy = pair_copy(0, extract, extract_in)
    extract_copy.start()
    extract_copy.wait()
    slab[chip] = extract[core] + extract_in[...]

    def gather(phase, buffer):
        started = []
        numbers = iter(range(40))

        def send(piece_of, axis, way):
            number = next(numbers)
            mine_at, theirs_at = piece_of(0), piece_of(way)
            sent = pltpu.make_async_remote_copy(
                src_ref=buffer.at[mine_at],
                dst_ref=buffer.at[mine_at],
                send_sem=plane_send.at[phase, number],
                recv_sem=plane_recv.at[phase, number],
                device_id=chip_device(*step(axis, way)),
                device_id_type=MESH,
            )
            sent.start()
            arrives = pltpu.make_async_remote_copy(
                src_ref=buffer.at[theirs_at],
                dst_ref=buffer.at[theirs_at],
                send_sem=plane_send.at[phase, number],
                recv_sem=plane_recv.at[phase, number],
                device_id=chip_device(*step(axis, way)),
                device_id_type=MESH,
            )
            started.append(sent)
            return arrives

        ways = (1, -1)
        halves = (0, 1)
        along_first = {}
        for half in halves:
            for way in ways:
                along_first[half, way] = send(
                    lambda back, half=half: half_piece(place(half, -back, 0), half), half, way)
        along_second = {}

        def send_second(half, offset):
            for way in ways:
                along_second[half, offset, way] = send(
                    lambda back: half_piece(place(half, offset, -back), half), 1 - half, way)

        for half in halves:
            send_second(half, 0)
        far_first = {}
        for half in halves:
            for way in ways:
                along_first[half, way].wait_recv()
                quarter = 0 if way == 1 else 1
                far_first[half, way] = send(
                    lambda back: quarter_piece(place(half, -way - back, 0), half, quarter), half, way)
                send_second(half, -way)
        for half in halves:
            for way in ways:
                far_first[half, way].wait_recv()
            send_second(half, 2)
        far_second = []
        for offset in (0, -1, 1, 2):
            for half in halves:
                for way in ways:
                    along_second[half, offset, way].wait_recv()
                    quarter = 0 if way == 1 else 1
                    far_second.append(send(
                        lambda back: quarter_piece(place(half, offset, -way - back), half, quarter),
                        1 - half, way))
        for arrives in far_second:
            arrives.wait_recv()
        return started

    def product(buffer):
        part[...] = jnp.zeros_like(part)

        def add(index, carry):
            left = buffer[index]
            for side in (0, 1):
                part[side] += jnp.dot(
                    left, panel[index, :, side * PANEL:(side + 1) * PANEL], preferred_element_type=F32)
            return carry

        lax.fori_loop(0, CHIPS, add, 0)

    slab_sent = gather(0, slab)
    product(slab)
    square_copy = pair_copy(1, part, part_in)
    square_copy.start()
    square_copy.wait()
    square[...] = part[core] + part_in[...]
    square_low[chip] = square[...].astype(BF16)
    square_sent = gather(1, square_low)
    product(square_low)
    cube_copy = pair_copy(2, part, cube_in)
    cube_copy.start()
    cube_copy.wait()
    out_ref[...] = 3.0 * square[...] - 2.0 * (part[core] + cube_in[...])

    for side in (0, 1):
        @pl.when(jnp.logical_not(jnp.logical_and(stays, y_high == side)))
        def _():
            swap_copy(side, core).wait_send()

    def ring_sent(distance, carry):
        for way, part_index in both:
            ring_copy(way, distance, part_index).wait_send()
        return carry

    lax.fori_loop(1, 8, ring_sent, 0)
    for way, part_index in last:
        ring_copy(way, 8, part_index).wait_send()
    for sent in slab_sent + square_sent:
        sent.wait_send()


def local(density, reach, slab_start):
    dma = pltpu.SemaphoreType.DMA
    vmem = pl.BlockSpec(memory_space=pltpu.VMEM)
    smem = pl.BlockSpec(memory_space=pltpu.SMEM)
    return pl.pallas_call(
        kernel,
        out_shape=jax.ShapeDtypeStruct((PANEL, PANEL), F32),
        in_specs=[vmem, smem, smem],
        out_specs=vmem,
        scratch_shapes=[
            pltpu.VMEM((2, BLOCK, WIDE), BF16),
            pltpu.VMEM((PLANES, PANEL, WIDE), BF16),
            pltpu.VMEM((CHIPS, PANEL, PANEL), BF16),
            pltpu.VMEM((CHIPS, PANEL, PANEL), BF16),
            pltpu.VMEM((2, PANEL, PANEL), BF16),
            pltpu.VMEM((PANEL, PANEL), BF16),
            pltpu.VMEM((2, PANEL, PANEL), F32),
            pltpu.VMEM((PANEL, PANEL), F32),
            pltpu.VMEM((PANEL, PANEL), F32),
            pltpu.VMEM((PANEL, PANEL), F32),
            dma((2,)), dma((2,)),
            dma((2, 8, 2)), dma((2, 8, 2)),
            dma((3,)), dma((3,)),
            dma((2, 40)), dma((2, 40)),
        ],
        compiler_params=pltpu.CompilerParams(
            collective_id=0, has_side_effects=True, vmem_limit_bytes=40 * 1024 * 1024),
    )(density, reach, slab_start)


def solution(mesh):
    return jax.shard_map(
        local,
        mesh=mesh,
        in_specs=(P(("row", "rep"), "col"), P(), P()),
        out_specs=P("row", ("col", "rep")),
        check_vma=False,
    )
```

```python
import jax
import jax.numpy as jnp
from jax import lax
from jax.experimental import pallas as pl
from jax.experimental.pallas import tpu as pltpu
from jax.sharding import PartitionSpec as P

BLOCK = 128
PANEL = 256
WIDE = 512
PLANES = 16
CHIPS = 16
SIDE = 4
GROUP = 128
WAYS = (1, -1, 2)
BLOCKS = 64
MESH = pl.DeviceIdType.MESH
F32 = jnp.float32
BF16 = jnp.bfloat16


def rem(value, count):
    return lax.rem(value + count, count)


def kernel(
    density_hbm, reach_hbm, start_hbm, out_ref,
    density_ref, reach_ref, start_ref,
    staged, panel, slab, square_low, extract, extract_in, part, part_in, cube, cube_in, square,
    load_sem, swap_send, swap_recv, ring_send, ring_recv, pair_send, pair_recv, plane_send, plane_recv,
):
    z = lax.axis_index("row")
    col = lax.axis_index("col")
    rep = lax.axis_index("rep")
    x, y_low = lax.div(col, 2), lax.rem(col, 2)
    y_high, core = lax.div(rep, 2), lax.rem(rep, 2)
    y = y_high * 2 + y_low
    other = 1 - core

    def chip_device(x_to, y_to):
        return (z, x_to * 2 + lax.rem(y_to, 2), lax.div(y_to, 2) * 2 + core)

    def chip_index(x_to, y_to):
        return x_to * 4 + lax.rem(y_to, 2) * 2 + lax.div(y_to, 2)

    def step(axis, offset):
        if axis == 0:
            return rem(x + offset, SIDE), y
        return x, rem(y + offset, SIDE)

    def place(first, first_offset, second_offset):
        if first == 0:
            return chip_index(rem(x + first_offset, SIDE), rem(y + second_offset, SIDE))
        return chip_index(rem(x + second_offset, SIDE), rem(y + first_offset, SIDE))

    up = (rem(z + 1, PLANES), col, rep)
    down = (rem(z - 1, PLANES), col, rep)
    sibling = (z, col, y_high * 2 + other)
    chip = chip_index(x, y)

    barrier = pltpu.get_barrier_semaphore()
    partners = [up, down]
    for axis in (0, 1):
        for offset in (1, -1):
            partners.append(chip_device(*step(axis, offset)))
    partners.append(chip_device(*step(0, 2)))
    for offset in (1, 2, 3):
        partners.append((z, col, rem(rep + offset, 4)))
    for partner in partners:
        pl.semaphore_signal(barrier, inc=1, device_id=partner, device_id_type=MESH)

    loads = [
        pltpu.make_async_copy(reach_hbm, reach_ref, load_sem.at[0]),
        pltpu.make_async_copy(density_hbm, density_ref, load_sem.at[1]),
        pltpu.make_async_copy(start_hbm, start_ref, load_sem.at[2]),
    ]
    for load in loads:
        load.start()
    for load in loads:
        load.wait()
    own_block = z * 4 + rep
    own_reach = reach_ref[own_block]
    for block in range(8):
        column_block = col * 8 + block
        spread = lax.abs(column_block - own_block)
        spread = lax.min(spread, BLOCKS - spread)
        kept = spread <= lax.min(reach_ref[column_block], own_reach)
        scale = jnp.where(kept, 1.0, 0.0).astype(F32)
        values = density_ref[:, block * BLOCK:(block + 1) * BLOCK].astype(F32) * scale
        place_at = pl.ds((block % 4) * BLOCK, BLOCK)
        staged[block // 4, :, place_at] = values.astype(BF16)
    pl.semaphore_wait(barrier, len(partners))

    stays = y_high == core

    def swap_copy(side, sender, half):
        rows = half * 64
        return pltpu.make_async_remote_copy(
            src_ref=staged.at[side, pl.ds(rows, 64)],
            dst_ref=panel.at[z, pl.ds(sender * BLOCK + rows, 64)],
            send_sem=swap_send.at[side, half],
            recv_sem=swap_recv.at[sender, half],
            device_id=(z, col, side * 2 + y_high),
            device_id_type=MESH,
        )

    for side in (0, 1):
        is_own = jnp.logical_and(stays, y_high == side)

        @pl.when(jnp.logical_not(is_own))
        def _():
            for half in (0, 1):
                swap_copy(side, core, half).start()

        @pl.when(is_own)
        def _():
            panel[z, pl.ds(side * BLOCK, BLOCK), :] = staged[side]

    def ring_copy(way, distance, quarter):
        behind = distance - 1
        slot = rem(z - behind, PLANES) if way == 0 else rem(z + behind, PLANES)
        return pltpu.make_async_remote_copy(
            src_ref=panel.at[slot, pl.ds(quarter * 64, 64)],
            dst_ref=panel.at[slot, pl.ds(quarter * 64, 64)],
            send_sem=ring_send.at[way, behind, quarter],
            recv_sem=ring_recv.at[way, behind, quarter],
            device_id=up if way == 0 else down,
            device_id_type=MESH,
        )

    for quarter in range(4):
        sender = quarter // 2
        is_own = jnp.logical_and(stays, core == sender)

        @pl.when(jnp.logical_not(is_own))
        def _():
            swap_copy(sender, sender, quarter % 2).wait_recv()

        for way in (0, 1):
            ring_copy(way, 1, quarter).start()

    both = [(way, quarter) for quarter in range(4) for way in (0, 1)]
    last = [(0, 0), (1, 2), (0, 1), (1, 3)]

    def ring_step(distance, carry):
        for way, quarter in both:
            ring_copy(way, distance - 1, quarter).wait_recv()
            ring_copy(way, distance, quarter).start()
        return carry

    lax.fori_loop(2, 8, ring_step, 0)
    for way, quarter in last:
        ring_copy(way, 7, quarter).wait_recv()
        ring_copy(way, 8, quarter).start()
    for way, quarter in both:
        if (way, quarter) not in last:
            ring_copy(way, 7, quarter).wait_recv()
    for way, quarter in last:
        ring_copy(way, 8, quarter).wait_recv()

    first_row = start_ref[0] + z * PANEL
    first_block = lax.div(first_row, PANEL)
    inside = lax.rem(first_row, PANEL)
    mine = lax.rem(first_block, 2) == core
    held = jnp.where(mine, lax.div(first_block, 2), lax.min(lax.div(first_block + 1, 2), PLANES - 1))
    shift = jnp.where(mine, inside, inside - PANEL)
    block = panel[held]

    def pair_copy(index, source, target):
        return pltpu.make_async_remote_copy(
            src_ref=source,
            dst_ref=target,
            send_sem=pair_send.at[index],
            recv_sem=pair_recv.at[index],
            device_id=sibling,
            device_id_type=MESH,
        )

    groups = (0, 1)
    extracts = [pair_copy(g, extract.at[other, g], extract_in.at[g]) for g in groups]
    for g in groups:
        rows = lax.broadcasted_iota(jnp.int32, (GROUP, PANEL), 0) + g * GROUP
        columns = lax.broadcasted_iota(jnp.int32, (GROUP, PANEL), 1)
        pick = jnp.where(columns == rows + shift, 1.0, 0.0).astype(BF16)
        rows_out = jnp.dot(pick, block, preferred_element_type=F32).astype(BF16)
        extract[0, g] = rows_out[:, :PANEL]
        extract[1, g] = rows_out[:, PANEL:]
        extracts[g].start()

    class Gather:
        def __init__(self, phase, g, buffer):
            self.phase, self.g, self.buffer = phase, g, buffer
            self.count = 0
            self.sent = []
            self.first, self.second = {}, []

        def send(self, half, axis, way, mine, theirs):
            at = pl.ds(self.g * GROUP + half * 64, 64)
            target = chip_device(*step(axis, way))
            sems = dict(
                send_sem=plane_send.at[self.phase, self.g, self.count],
                recv_sem=plane_recv.at[self.phase, self.g, self.count],
                device_id=target, device_id_type=MESH)
            self.count += 1
            sent = pltpu.make_async_remote_copy(
                src_ref=self.buffer.at[mine, at], dst_ref=self.buffer.at[mine, at], **sems)
            sent.start()
            self.sent.append(sent)
            return pltpu.make_async_remote_copy(
                src_ref=self.buffer.at[theirs, at], dst_ref=self.buffer.at[theirs, at], **sems)

        def send_second(self, half, offset):
            for way in WAYS:
                self.second.append(self.send(
                    half, 1 - half, way, place(half, offset, 0), place(half, offset, -way)))

        def start(self):
            for way in WAYS:
                for half in (0, 1):
                    self.first[half, way] = self.send(
                        half, half, way, place(half, 0, 0), place(half, -way, 0))
            for half in (0, 1):
                self.send_second(half, 0)

        def middle(self):
            for way in WAYS:
                for half in (0, 1):
                    self.first[half, way].wait_recv()
                    self.send_second(half, -way)

        def finish(self):
            for arrives in self.second:
                arrives.wait_recv()

    def product(buffer, g, target):
        for first in range(0, CHIPS, 4):
            left = jnp.concatenate(
                [buffer[first + i, g * GROUP:(g + 1) * GROUP, :] for i in range(4)], axis=1)
            right = panel[first:first + 4].reshape(4 * PANEL, WIDE)
            for side in (0, 1):
                value = jnp.dot(
                    left, right[:, side * PANEL:(side + 1) * PANEL], preferred_element_type=F32)
                if first:
                    target[side, g] += value
                else:
                    target[side, g] = value

    slab_gathers = [Gather(0, g, slab) for g in groups]
    square_gathers = [Gather(1, g, square_low) for g in groups]
    squares = [pair_copy(2 + g, part.at[other, g], part_in.at[g]) for g in groups]
    cubes = [pair_copy(4 + g, cube.at[other, g], cube_in.at[g]) for g in groups]

    def slab_start(g):
        extracts[g].wait_recv()
        slab[chip, g * GROUP:(g + 1) * GROUP, :] = extract[core, g] + extract_in[g]
        slab_gathers[g].start()

    def square_part(g):
        slab_gathers[g].finish()
        product(slab, g, part)
        squares[g].start()

    def square_start(g):
        squares[g].wait_recv()
        square[g] = part[core, g] + part_in[g]
        square_low[chip, g * GROUP:(g + 1) * GROUP, :] = square[g].astype(BF16)
        square_gathers[g].start()

    def cube_part(g):
        square_gathers[g].finish()
        product(square_low, g, cube)
        cubes[g].start()

    def result(g):
        cubes[g].wait_recv()
        out_ref[g * GROUP:(g + 1) * GROUP, :] = 3.0 * square[g] - 2.0 * (cube[core, g] + cube_in[g])

    slab_start(0)
    slab_start(1)
    slab_gathers[0].middle()
    slab_gathers[1].middle()
    square_part(0)
    square_start(0)
    square_part(1)
    square_gathers[0].middle()
    square_start(1)
    square_gathers[1].middle()
    cube_part(0)
    cube_part(1)
    result(0)
    result(1)

    for side in (0, 1):
        @pl.when(jnp.logical_not(jnp.logical_and(stays, y_high == side)))
        def _():
            for half in (0, 1):
                swap_copy(side, core, half).wait_send()

    def ring_sent(distance, carry):
        for way, quarter in both:
            ring_copy(way, distance, quarter).wait_send()
        return carry

    lax.fori_loop(1, 8, ring_sent, 0)
    for way, quarter in last:
        ring_copy(way, 8, quarter).wait_send()
    for copy in extracts + squares + cubes:
        copy.wait_send()
    for gather in slab_gathers + square_gathers:
        for sent in gather.sent:
            sent.wait_send()


def local(density, reach, slab_start):
    dma = pltpu.SemaphoreType.DMA
    vmem = pl.BlockSpec(memory_space=pltpu.VMEM)
    hbm = pl.BlockSpec(memory_space=pltpu.HBM)
    return pl.pallas_call(
        kernel,
        out_shape=jax.ShapeDtypeStruct((PANEL, PANEL), F32),
        in_specs=[hbm, hbm, hbm],
        out_specs=vmem,
        scratch_shapes=[
            pltpu.VMEM((BLOCK, 8 * BLOCK), BF16),
            pltpu.SMEM((BLOCKS,), jnp.int32),
            pltpu.SMEM((1,), jnp.int32),
            pltpu.VMEM((2, BLOCK, WIDE), BF16),
            pltpu.VMEM((PLANES, PANEL, WIDE), BF16),
            pltpu.VMEM((CHIPS, PANEL, PANEL), BF16),
            pltpu.VMEM((CHIPS, PANEL, PANEL), BF16),
            pltpu.VMEM((2, 2, GROUP, PANEL), BF16),
            pltpu.VMEM((2, GROUP, PANEL), BF16),
            pltpu.VMEM((2, 2, GROUP, PANEL), F32),
            pltpu.VMEM((2, GROUP, PANEL), F32),
            pltpu.VMEM((2, 2, GROUP, PANEL), F32),
            pltpu.VMEM((2, GROUP, PANEL), F32),
            pltpu.VMEM((2, GROUP, PANEL), F32),
            dma((3,)),
            dma((2, 2)), dma((2, 2)),
            dma((2, 8, 4)), dma((2, 8, 4)),
            dma((6,)), dma((6,)),
            dma((2, 2, 30)), dma((2, 2, 30)),
        ],
        compiler_params=pltpu.CompilerParams(
            collective_id=0, has_side_effects=True, vmem_limit_bytes=40 * 1024 * 1024),
    )(density, reach, slab_start)


def solution(mesh):
    return jax.shard_map(
        local,
        mesh=mesh,
        in_specs=(P(("row", "rep"), "col"), P(), P()),
        out_specs=P("row", ("col", "rep")),
        check_vma=False,
    )
```

```python
import jax
import jax.numpy as jnp
from jax import lax
from jax.experimental import pallas as pl
from jax.experimental.pallas import tpu as pltpu
from jax.sharding import PartitionSpec as P

BLOCK = 128
PANEL = 256
WIDE = 512
PLANES = 16
CHIPS = 16
SIDE = 4
GROUPS = 2
GROUP = PANEL // GROUPS
HALF = GROUP // 2
ORDER = (0, 2, 1, 3)
WAYS = (1, -1, 2)
OFFSETS = (0, -1, 1, -2)
BLOCKS = 64
MESH = pl.DeviceIdType.MESH
F32 = jnp.float32
BF16 = jnp.bfloat16


def rem(value, count):
    return lax.rem(value + count, count)


def kernel(
    density_hbm, reach_hbm, start_hbm, out_ref,
    density_ref, reach_ref, start_ref,
    staged, panel, slab, square_low, extract, extract_in, part, part_in, cube, cube_in, square,
    load_sem, swap_send, swap_recv, ring_send, ring_recv, pair_send, pair_recv, plane_send, plane_recv,
):
    z = lax.axis_index("row")
    col = lax.axis_index("col")
    rep = lax.axis_index("rep")
    x, y_low = lax.div(col, 2), lax.rem(col, 2)
    y_high, core = lax.div(rep, 2), lax.rem(rep, 2)
    y = y_high * 2 + y_low
    other = 1 - core

    def chip_device(x_to, y_to):
        return (z, x_to * 2 + lax.rem(y_to, 2), lax.div(y_to, 2) * 2 + core)

    def chip_index(x_to, y_to):
        return x_to * 4 + lax.rem(y_to, 2) * 2 + lax.div(y_to, 2)

    def step(axis, offset):
        if axis == 0:
            return rem(x + offset, SIDE), y
        return x, rem(y + offset, SIDE)

    def place(first, first_offset, second_offset):
        if first == 0:
            return chip_index(rem(x + first_offset, SIDE), rem(y + second_offset, SIDE))
        return chip_index(rem(x + second_offset, SIDE), rem(y + first_offset, SIDE))

    up = (rem(z + 1, PLANES), col, rep)
    down = (rem(z - 1, PLANES), col, rep)
    sibling = (z, col, y_high * 2 + other)
    chip = chip_index(x, y)

    barrier = pltpu.get_barrier_semaphore()
    partners = [up, down]
    for axis in (0, 1):
        for offset in (1, -1):
            partners.append(chip_device(*step(axis, offset)))
    partners.append(chip_device(*step(0, 2)))
    for offset in (1, 2, 3):
        partners.append((z, col, rem(rep + offset, 4)))
    for partner in partners:
        pl.semaphore_signal(barrier, inc=1, device_id=partner, device_id_type=MESH)

    loads = [
        pltpu.make_async_copy(reach_hbm, reach_ref, load_sem.at[0]),
        pltpu.make_async_copy(density_hbm, density_ref, load_sem.at[1]),
        pltpu.make_async_copy(start_hbm, start_ref, load_sem.at[2]),
    ]
    for load in loads:
        load.start()
    for load in loads:
        load.wait()
    own_block = z * 4 + rep
    own_reach = reach_ref[own_block]
    for block in range(8):
        column_block = col * 8 + block
        spread = lax.abs(column_block - own_block)
        spread = lax.min(spread, BLOCKS - spread)
        kept = spread <= lax.min(reach_ref[column_block], own_reach)
        scale = jnp.where(kept, 1.0, 0.0).astype(F32)
        values = density_ref[:, block * BLOCK:(block + 1) * BLOCK].astype(F32) * scale
        place_at = pl.ds(ORDER[block % 4] * BLOCK, BLOCK)
        staged[block // 4, :, place_at] = values.astype(BF16)
    pl.semaphore_wait(barrier, len(partners))

    def swap_copy(half):
        rows = half * 64
        return pltpu.make_async_remote_copy(
            src_ref=staged.at[1 - y_high, pl.ds(rows, 64)],
            dst_ref=panel.at[z, y_high, pl.ds(rows, 64)],
            send_sem=swap_send.at[half],
            recv_sem=swap_recv.at[half],
            device_id=(z, col, (1 - y_high) * 2 + core),
            device_id_type=MESH,
        )

    for half in (0, 1):
        swap_copy(half).start()
    panel[z, y_high] = staged[y_high]

    def ring_copy(way, distance, quarter):
        behind = distance - 1
        slot = rem(z - behind, PLANES) if way == 0 else rem(z + behind, PLANES)
        where = panel.at[slot, y_high if quarter < 2 else 1 - y_high, pl.ds((quarter % 2) * 64, 64)]
        return pltpu.make_async_remote_copy(
            src_ref=where,
            dst_ref=where,
            send_sem=ring_send.at[way, behind, quarter],
            recv_sem=ring_recv.at[way, behind, quarter],
            device_id=up if way == 0 else down,
            device_id_type=MESH,
        )

    for quarter in range(4):
        if quarter >= 2:
            swap_copy(quarter - 2).wait_recv()
        for way in (0, 1):
            ring_copy(way, 1, quarter).start()

    both = [(way, quarter) for quarter in range(4) for way in (0, 1)]
    last = [(0, 0), (1, 2), (0, 1), (1, 3)]

    def ring_step(distance, carry):
        for way, quarter in both:
            ring_copy(way, distance - 1, quarter).wait_recv()
            ring_copy(way, distance, quarter).start()
        return carry

    lax.fori_loop(2, 8, ring_step, 0)
    for way, quarter in last:
        ring_copy(way, 7, quarter).wait_recv()
        ring_copy(way, 8, quarter).start()
    for way, quarter in both:
        if (way, quarter) not in last:
            ring_copy(way, 7, quarter).wait_recv()
    for way, quarter in last:
        ring_copy(way, 8, quarter).wait_recv()

    first_row = start_ref[0] + z * PANEL
    first_block = lax.div(first_row, BLOCK)
    inside = lax.rem(first_row, BLOCK)
    mine = lax.rem(first_block, 2) == core
    wanted = jnp.where(mine, lax.div(first_block, 2), lax.div(first_block + 1, 2))
    held = lax.min(wanted, 2 * PLANES - 2)
    past = (wanted - held) * BLOCK
    flat = panel.reshape(2 * PLANES, BLOCK, WIDE)
    block = flat[pl.ds(held, 2)].reshape(PANEL, WIDE)

    def pair_copy(index, source, target):
        return pltpu.make_async_remote_copy(
            src_ref=source,
            dst_ref=target,
            send_sem=pair_send.at[index],
            recv_sem=pair_recv.at[index],
            device_id=sibling,
            device_id_type=MESH,
        )

    groups = range(GROUPS)
    extracts = [pair_copy(g, extract.at[other, g], extract_in.at[g]) for g in groups]
    for g in groups:
        rows = lax.broadcasted_iota(jnp.int32, (GROUP, PANEL), 0) + g * GROUP
        columns = lax.broadcasted_iota(jnp.int32, (GROUP, PANEL), 1)
        seen = rows + inside
        middle = jnp.logical_and(seen >= BLOCK, seen < 2 * BLOCK)
        wants = jnp.where(jnp.logical_and(mine, seen < BLOCK), seen, seen - BLOCK) + past
        taken = jnp.logical_and(columns == wants, middle != mine)
        pick = jnp.where(taken, 1.0, 0.0).astype(BF16)
        rows_out = jnp.dot(pick, block, preferred_element_type=F32).astype(BF16)
        extract[0, g] = rows_out[:, :PANEL]
        extract[1, g] = rows_out[:, PANEL:]
        extracts[g].start()

    class Gather:
        def __init__(self, phase, g, buffer):
            self.phase, self.g, self.buffer = phase, g, buffer
            self.count = 0
            self.sent = []
            self.first, self.second = {}, {}

        def send(self, half, axis, way, mine, theirs):
            at = pl.ds(self.g * GROUP + half * HALF, HALF)
            target = chip_device(*step(axis, way))
            sems = dict(
                send_sem=plane_send.at[self.phase, self.g, self.count],
                recv_sem=plane_recv.at[self.phase, self.g, self.count],
                device_id=target, device_id_type=MESH)
            self.count += 1
            sent = pltpu.make_async_remote_copy(
                src_ref=self.buffer.at[mine, at], dst_ref=self.buffer.at[mine, at], **sems)
            sent.start()
            self.sent.append(sent)
            return pltpu.make_async_remote_copy(
                src_ref=self.buffer.at[theirs, at], dst_ref=self.buffer.at[theirs, at], **sems)

        def send_second(self, half, offset):
            for way in (1, -1):
                self.second[half, offset, way] = self.send(
                    half, 1 - half, way, place(half, offset, 0), place(half, offset, -way))

        def start(self):
            for way in WAYS:
                for half in (0, 1):
                    self.first[half, way] = self.send(
                        half, half, way, place(half, 0, 0), place(half, -way, 0))
            for half in (0, 1):
                self.send_second(half, 0)

        def middle(self):
            for way in WAYS:
                for half in (0, 1):
                    self.first[half, way].wait_recv()
                    self.send_second(half, -way)

        def forward(self):
            for offset in OFFSETS:
                way = 1 if offset in (0, -2) else -1
                for half in (0, 1):
                    self.second.pop((half, offset, way)).wait_recv()
                    self.second[half, offset] = self.send(
                        half, 1 - half, way, place(half, offset, -way), place(half, offset, -2 * way))

        def finish(self):
            for arrives in self.second.values():
                arrives.wait_recv()

    def product(buffer, g, target):
        for first in range(0, CHIPS, 4):
            left = jnp.concatenate(
                [buffer[first + i, g * GROUP:(g + 1) * GROUP, :] for i in range(4)], axis=1)
            right = panel[first:first + 4].reshape(4 * PANEL, WIDE)
            for side in (0, 1):
                value = jnp.dot(
                    left, right[:, side * PANEL:(side + 1) * PANEL], preferred_element_type=F32)
                if first:
                    target[side, g] += value
                else:
                    target[side, g] = value

    slab_gathers = [Gather(0, g, slab) for g in groups]
    square_gathers = [Gather(1, g, square_low) for g in groups]
    squares = [pair_copy(GROUPS + g, part.at[other, g], part_in.at[g]) for g in groups]
    cubes = [pair_copy(2 * GROUPS + g, cube.at[other, g], cube_in.at[g]) for g in groups]

    def slab_start(g):
        extracts[g].wait_recv()
        slab[chip, g * GROUP:(g + 1) * GROUP, :] = extract[core, g] + extract_in[g]
        slab_gathers[g].start()

    def square_part(g):
        slab_gathers[g].finish()
        product(slab, g, part)
        squares[g].start()

    def square_start(g):
        squares[g].wait_recv()
        square[g] = part[core, g] + part_in[g]
        square_low[chip, g * GROUP:(g + 1) * GROUP, :] = square[g].astype(BF16)
        square_gathers[g].start()

    def cube_part(g):
        square_gathers[g].finish()
        squares[g].wait_send()
        product(square_low, g, part)
        for colour in (0, 1):
            own = jnp.where(core == colour, 3.0, 0.0)
            value = own * square[g] - 2.0 * part[colour, g]
            for side in (0, 1):
                cube[side, g, :, colour * BLOCK:(colour + 1) * BLOCK] = value[:, side * BLOCK:(side + 1) * BLOCK]
        cubes[g].start()

    def result(g):
        cubes[g].wait_recv()
        out_ref[g * GROUP:(g + 1) * GROUP, :] = cube[core, g] + cube_in[g]

    slab_start(0)
    slab_start(1)
    slab_gathers[0].middle()
    slab_gathers[1].middle()
    slab_gathers[0].forward()
    slab_gathers[1].forward()
    square_part(0)
    square_start(0)
    square_part(1)
    square_start(1)
    square_gathers[0].middle()
    square_gathers[1].middle()
    square_gathers[0].forward()
    square_gathers[1].forward()
    cube_part(0)
    cube_part(1)
    result(0)
    result(1)

    for half in (0, 1):
        swap_copy(half).wait_send()

    def ring_sent(distance, carry):
        for way, quarter in both:
            ring_copy(way, distance, quarter).wait_send()
        return carry

    lax.fori_loop(1, 8, ring_sent, 0)
    for way, quarter in last:
        ring_copy(way, 8, quarter).wait_send()
    for copy in extracts + cubes:
        copy.wait_send()
    for gather in slab_gathers + square_gathers:
        for sent in gather.sent:
            sent.wait_send()


def local(density, reach, slab_start):
    dma = pltpu.SemaphoreType.DMA
    vmem = pl.BlockSpec(memory_space=pltpu.VMEM)
    hbm = pl.BlockSpec(memory_space=pltpu.HBM)
    return pl.pallas_call(
        kernel,
        out_shape=jax.ShapeDtypeStruct((PANEL, PANEL), F32),
        in_specs=[hbm, hbm, hbm],
        out_specs=vmem,
        scratch_shapes=[
            pltpu.VMEM((BLOCK, 8 * BLOCK), BF16),
            pltpu.SMEM((BLOCKS,), jnp.int32),
            pltpu.SMEM((1,), jnp.int32),
            pltpu.VMEM((2, BLOCK, WIDE), BF16),
            pltpu.VMEM((PLANES, 2, BLOCK, WIDE), BF16),
            pltpu.VMEM((CHIPS, PANEL, PANEL), BF16),
            pltpu.VMEM((CHIPS, PANEL, PANEL), BF16),
            pltpu.VMEM((2, GROUPS, GROUP, PANEL), BF16),
            pltpu.VMEM((GROUPS, GROUP, PANEL), BF16),
            pltpu.VMEM((2, GROUPS, GROUP, PANEL), F32),
            pltpu.VMEM((GROUPS, GROUP, PANEL), F32),
            pltpu.VMEM((2, GROUPS, GROUP, PANEL), F32),
            pltpu.VMEM((GROUPS, GROUP, PANEL), F32),
            pltpu.VMEM((GROUPS, GROUP, PANEL), F32),
            dma((3,)),
            dma((2,)), dma((2,)),
            dma((2, 8, 4)), dma((2, 8, 4)),
            dma((3 * GROUPS,)), dma((3 * GROUPS,)),
            dma((2, GROUPS, 30)), dma((2, GROUPS, 30)),
        ],
        compiler_params=pltpu.CompilerParams(
            collective_id=0, has_side_effects=True, vmem_limit_bytes=40 * 1024 * 1024),
    )(density, reach, slab_start)


def solution(mesh):
    return jax.shard_map(
        local,
        mesh=mesh,
        in_specs=(P(("row", "rep"), "col"), P(), P()),
        out_specs=P("row", ("col", "rep")),
        check_vma=False,
    )
```

```python
import jax
import jax.numpy as jnp
from jax import lax
from jax.experimental import pallas as pl
from jax.experimental.pallas import tpu as pltpu
from jax.sharding import PartitionSpec as P

BLOCK = 128
PANEL = 256
WIDE = 512
PLANES = 16
CHIPS = 16
SIDE = 4
GROUPS = 2
GROUP = PANEL // GROUPS
HALF = GROUP // 2
ORDER = (0, 2, 1, 3)
WAYS = (1, -1, 2)
FIRST = (1, -1, 2)
OFFSETS = (0, -1, 1, -2)
BLOCKS = 64
MESH = pl.DeviceIdType.MESH
F32 = jnp.float32
BF16 = jnp.bfloat16


def rem(value, count):
    return lax.rem(value + count, count)


def kernel(
    density_hbm, reach_hbm, start_hbm, out_ref,
    density_ref, reach_ref, start_ref,
    staged, panel, slab, square_low, extract, extract_in, part, part_in, cube, cube_in, square,
    load_sem, swap_send, swap_recv, ring_send, ring_recv, pair_send, pair_recv, plane_send, plane_recv,
):
    z = lax.axis_index("row")
    col = lax.axis_index("col")
    rep = lax.axis_index("rep")
    x, y_low = lax.div(col, 2), lax.rem(col, 2)
    y_high, core = lax.div(rep, 2), lax.rem(rep, 2)
    y = y_high * 2 + y_low
    other = 1 - core

    def chip_device(x_to, y_to):
        return (z, x_to * 2 + lax.rem(y_to, 2), lax.div(y_to, 2) * 2 + core)

    def chip_index(x_to, y_to):
        return x_to * 4 + lax.rem(y_to, 2) * 2 + lax.div(y_to, 2)

    def step(axis, offset):
        if axis == 0:
            return rem(x + offset, SIDE), y
        return x, rem(y + offset, SIDE)

    def place(first, first_offset, second_offset):
        if first == 0:
            return chip_index(rem(x + first_offset, SIDE), rem(y + second_offset, SIDE))
        return chip_index(rem(x + second_offset, SIDE), rem(y + first_offset, SIDE))

    up = (rem(z + 1, PLANES), col, rep)
    down = (rem(z - 1, PLANES), col, rep)
    sibling = (z, col, y_high * 2 + other)
    chip = chip_index(x, y)

    barrier = pltpu.get_barrier_semaphore()
    partners = [up, down]
    for axis in (0, 1):
        for offset in (1, -1):
            partners.append(chip_device(*step(axis, offset)))
    partners.append(chip_device(*step(0, 2)))
    for offset in (1, 2, 3):
        partners.append((z, col, rem(rep + offset, 4)))
    for partner in partners:
        pl.semaphore_signal(barrier, inc=1, device_id=partner, device_id_type=MESH)

    loads = [
        pltpu.make_async_copy(reach_hbm, reach_ref, load_sem.at[0]),
        pltpu.make_async_copy(density_hbm, density_ref, load_sem.at[1]),
        pltpu.make_async_copy(start_hbm, start_ref, load_sem.at[2]),
    ]
    for load in loads:
        load.start()
    for load in loads:
        load.wait()
    own_block = z * 4 + rep
    own_reach = reach_ref[own_block]
    for block in range(8):
        column_block = col * 8 + block
        spread = lax.abs(column_block - own_block)
        spread = lax.min(spread, BLOCKS - spread)
        kept = spread <= lax.min(reach_ref[column_block], own_reach)
        scale = jnp.where(kept, 1.0, 0.0).astype(F32)
        values = density_ref[:, block * BLOCK:(block + 1) * BLOCK].astype(F32) * scale
        place_at = pl.ds(ORDER[block % 4] * BLOCK, BLOCK)
        staged[block // 4, :, place_at] = values.astype(BF16)
    pl.semaphore_wait(barrier, len(partners))

    def swap_copy(half):
        rows = half * 64
        return pltpu.make_async_remote_copy(
            src_ref=staged.at[1 - y_high, pl.ds(rows, 64)],
            dst_ref=panel.at[z, y_high, pl.ds(rows, 64)],
            send_sem=swap_send.at[half],
            recv_sem=swap_recv.at[half],
            device_id=(z, col, (1 - y_high) * 2 + core),
            device_id_type=MESH,
        )

    for half in (0, 1):
        swap_copy(half).start()
    panel[z, y_high] = staged[y_high]

    def ring_copy(way, distance, quarter):
        behind = distance - 1
        slot = rem(z - behind, PLANES) if way == 0 else rem(z + behind, PLANES)
        where = panel.at[slot, y_high if quarter < 2 else 1 - y_high, pl.ds((quarter % 2) * 64, 64)]
        return pltpu.make_async_remote_copy(
            src_ref=where,
            dst_ref=where,
            send_sem=ring_send,
            recv_sem=ring_recv.at[way, behind, quarter],
            device_id=up if way == 0 else down,
            device_id_type=MESH,
        )

    for quarter in range(4):
        if quarter >= 2:
            swap_copy(quarter - 2).wait_recv()
        for way in (0, 1):
            ring_copy(way, 1, quarter).start()

    both = [(way, quarter) for quarter in range(4) for way in (0, 1)]
    last = [(0, 0), (1, 2), (0, 1), (1, 3)]

    def ring_step(distance, carry):
        for way, quarter in both:
            ring_copy(way, distance - 1, quarter).wait_recv()
            ring_copy(way, distance, quarter).start()
        return carry

    lax.fori_loop(2, 8, ring_step, 0)
    for way, quarter in last:
        ring_copy(way, 7, quarter).wait_recv()
        ring_copy(way, 8, quarter).start()
    for way, quarter in both:
        if (way, quarter) not in last:
            ring_copy(way, 7, quarter).wait_recv()
    for way, quarter in last:
        ring_copy(way, 8, quarter).wait_recv()

    first_row = start_ref[0] + z * PANEL
    first_block = lax.div(first_row, BLOCK)
    inside = lax.rem(first_row, BLOCK)
    mine = lax.rem(first_block, 2) == core
    wanted = jnp.where(mine, lax.div(first_block, 2), lax.div(first_block + 1, 2))
    held = lax.min(wanted, 2 * PLANES - 2)
    past = (wanted - held) * BLOCK
    flat = panel.reshape(2 * PLANES, BLOCK, WIDE)
    block = flat[pl.ds(held, 2)].reshape(PANEL, WIDE)

    def pair_copy(index, source, target):
        return pltpu.make_async_remote_copy(
            src_ref=source,
            dst_ref=target,
            send_sem=pair_send.at[index],
            recv_sem=pair_recv.at[index],
            device_id=sibling,
            device_id_type=MESH,
        )

    groups = range(GROUPS)
    extracts = [pair_copy(g, extract.at[other, g], extract_in.at[g]) for g in groups]
    for g in groups:
        rows = lax.broadcasted_iota(jnp.int32, (GROUP, PANEL), 0) + g * GROUP
        columns = lax.broadcasted_iota(jnp.int32, (GROUP, PANEL), 1)
        seen = rows + inside
        middle = jnp.logical_and(seen >= BLOCK, seen < 2 * BLOCK)
        wants = jnp.where(jnp.logical_and(mine, seen < BLOCK), seen, seen - BLOCK) + past
        taken = jnp.logical_and(columns == wants, middle != mine)
        pick = jnp.where(taken, 1.0, 0.0).astype(BF16)
        rows_out = jnp.dot(pick, block, preferred_element_type=F32).astype(BF16)
        extract[0, g] = rows_out[:, :PANEL]
        extract[1, g] = rows_out[:, PANEL:]
        extracts[g].start()

    class Gather:
        def __init__(self, phase, g, buffer):
            self.phase, self.g, self.buffer = phase, g, buffer
            self.count = 0
            self.first, self.second = {}, {}

        def send(self, half, axis, way, mine, theirs, number=None):
            at = pl.ds(self.g * GROUP + half * HALF, HALF)
            if number is None:
                number = self.count
                self.count += 1
            sems = dict(
                send_sem=plane_send.at[self.phase],
                recv_sem=plane_recv.at[self.phase, self.g, number],
                device_id=chip_device(*step(axis, way)), device_id_type=MESH)
            pltpu.make_async_remote_copy(
                src_ref=self.buffer.at[mine, at], dst_ref=self.buffer.at[mine, at], **sems).start()

            def arrives():
                pltpu.make_async_remote_copy(
                    src_ref=self.buffer.at[theirs, at], dst_ref=self.buffer.at[theirs, at], **sems).wait_recv()

            return arrives

        def send_second(self, half, offset):
            onward = 1 if offset in (0, -2) else -1
            for way in (1, -1):
                self.second[half, offset, way] = self.send(
                    half, 1 - half, way, place(half, offset, 0), place(half, offset, -way),
                    None if way == onward else 14)

        def start(self):
            for way in FIRST:
                for half in (0, 1):
                    self.first[half, way] = self.send(
                        half, half, way, place(half, 0, 0), place(half, -way, 0))
            for half in (0, 1):
                self.send_second(half, 0)

        def middle(self):
            for way in WAYS:
                for half in (0, 1):
                    self.first[half, way]()
                    self.send_second(half, -way)

        def forward(self):
            for offset in OFFSETS:
                way = 1 if offset in (0, -2) else -1
                for half in (0, 1):
                    self.second[half, offset, way]()
                    self.send(half, 1 - half, way, place(half, offset, -way), place(half, offset, -2 * way), 15)

        def all_of(self, number):
            pltpu.make_async_remote_copy(
                src_ref=self.buffer.at[pl.ds(0, 2), pl.ds(0, PANEL)],
                dst_ref=self.buffer.at[pl.ds(0, 2), pl.ds(0, PANEL)],
                send_sem=plane_send.at[self.phase],
                recv_sem=plane_recv.at[self.phase, self.g, number],
                device_id=sibling, device_id_type=MESH).wait_recv()

        def near(self):
            self.all_of(14)

        def finish(self):
            self.all_of(15)

    NEAR = [(dx, dy) for dx in (0, 1, -1) for dy in (0, 1, -1)]
    FAR = [(2, dy) for dy in (0, 1, -1, 2)] + [(dx, 2) for dx in (0, 1, -1)]

    def product(buffer, g, target, offsets, first):
        rows = pl.ds(g * GROUP, GROUP)
        value = None
        indices = [place(0, dx, dy) for dx, dy in offsets]
        left = jnp.concatenate([buffer[index, rows, :] for index in indices], axis=1)
        right = jnp.concatenate([panel[index].reshape(PANEL, WIDE) for index in indices], axis=0)
        value = jnp.dot(left, right, preferred_element_type=F32)
        for side in (0, 1):
            half = value[:, side * PANEL:(side + 1) * PANEL]
            target[side, g] = half if first else target[side, g] + half

    def all_sent(array, semaphore):
        pltpu.make_async_remote_copy(
            src_ref=array.at[pl.ds(0, PLANES - 1)],
            dst_ref=array.at[pl.ds(0, PLANES - 1)],
            send_sem=semaphore,
            recv_sem=semaphore,
            device_id=sibling,
            device_id_type=MESH,
        ).wait_send()

    slab_gathers = [Gather(0, g, slab) for g in groups]
    square_gathers = [Gather(1, g, square_low) for g in groups]
    squares = [pair_copy(GROUPS + g, part.at[other, g], part_in.at[g]) for g in groups]
    cubes = [pair_copy(2 * GROUPS + g, cube.at[other, g], cube_in.at[g]) for g in groups]

    def slab_start(g):
        extracts[g].wait_recv()
        slab[chip, g * GROUP:(g + 1) * GROUP, :] = extract[core, g] + extract_in[g]
        slab_gathers[g].start()

    def square_near(g):
        slab_gathers[g].near()
        product(slab, g, part, NEAR, True)

    def square_part(g):
        slab_gathers[g].finish()
        product(slab, g, part, FAR, False)
        squares[g].start()

    def square_start(g):
        squares[g].wait_recv()
        square[g] = part[core, g] + part_in[g]
        square_low[chip, g * GROUP:(g + 1) * GROUP, :] = square[g].astype(BF16)
        square_gathers[g].start()

    def cube_near(g):
        squares[g].wait_send()
        square_gathers[g].near()
        product(square_low, g, part, NEAR, True)

    def cube_part(g):
        square_gathers[g].finish()
        product(square_low, g, part, FAR, False)
        for colour in (0, 1):
            own = jnp.where(core == colour, 3.0, 0.0)
            value = own * square[g] - 2.0 * part[colour, g]
            for side in (0, 1):
                cube[side, g, :, colour * BLOCK:(colour + 1) * BLOCK] = value[:, side * BLOCK:(side + 1) * BLOCK]
        cubes[g].start()

    def result(g):
        cubes[g].wait_recv()
        out_ref[g * GROUP:(g + 1) * GROUP, :] = cube[core, g] + cube_in[g]

    slab_start(0)
    slab_start(1)
    all_sent(panel, ring_send)
    for copy in [swap_copy(0), swap_copy(1)] + extracts:
        copy.wait_send()
    slab_gathers[0].middle()
    slab_gathers[1].middle()
    slab_gathers[0].forward()
    slab_gathers[1].forward()
    square_near(0)
    square_near(1)
    square_part(0)
    square_start(0)
    square_part(1)
    square_start(1)
    all_sent(slab, plane_send.at[0])
    square_gathers[0].middle()
    square_gathers[1].middle()
    square_gathers[0].forward()
    square_gathers[1].forward()
    cube_near(0)
    cube_near(1)
    cube_part(0)
    cube_part(1)
    all_sent(square_low, plane_send.at[1])
    result(0)
    result(1)

    for copy in cubes:
        copy.wait_send()


def local(density, reach, slab_start):
    dma = pltpu.SemaphoreType.DMA
    vmem = pl.BlockSpec(memory_space=pltpu.VMEM)
    hbm = pl.BlockSpec(memory_space=pltpu.HBM)
    return pl.pallas_call(
        kernel,
        out_shape=jax.ShapeDtypeStruct((PANEL, PANEL), F32),
        in_specs=[hbm, hbm, hbm],
        out_specs=vmem,
        scratch_shapes=[
            pltpu.VMEM((BLOCK, 8 * BLOCK), BF16),
            pltpu.SMEM((BLOCKS,), jnp.int32),
            pltpu.SMEM((1,), jnp.int32),
            pltpu.VMEM((2, BLOCK, WIDE), BF16),
            pltpu.VMEM((PLANES, 2, BLOCK, WIDE), BF16),
            pltpu.VMEM((CHIPS, PANEL, PANEL), BF16),
            pltpu.VMEM((CHIPS, PANEL, PANEL), BF16),
            pltpu.VMEM((2, GROUPS, GROUP, PANEL), BF16),
            pltpu.VMEM((GROUPS, GROUP, PANEL), BF16),
            pltpu.VMEM((2, GROUPS, GROUP, PANEL), F32),
            pltpu.VMEM((GROUPS, GROUP, PANEL), F32),
            pltpu.VMEM((2, GROUPS, GROUP, PANEL), F32),
            pltpu.VMEM((GROUPS, GROUP, PANEL), F32),
            pltpu.VMEM((GROUPS, GROUP, PANEL), F32),
            dma((3,)),
            dma((2,)), dma((2,)),
            dma, dma((2, 8, 4)),
            dma((3 * GROUPS,)), dma((3 * GROUPS,)),
            dma((2,)), dma((2, GROUPS, 16)),
        ],
        compiler_params=pltpu.CompilerParams(
            collective_id=0, has_side_effects=True, vmem_limit_bytes=40 * 1024 * 1024),
    )(density, reach, slab_start)


def solution(mesh):
    return jax.shard_map(
        local,
        mesh=mesh,
        in_specs=(P(("row", "rep"), "col"), P(), P()),
        out_specs=P("row", ("col", "rep")),
        check_vma=False,
    )
```

```python
import jax
import jax.numpy as jnp
from jax import lax
from jax.experimental import pallas as pl
from jax.experimental.pallas import tpu as pltpu
from jax.sharding import PartitionSpec as P

BLOCK = 128
PANEL = 256
WIDE = 512
PLANES = 16
CHIPS = 16
SIDE = 4
GROUPS = 2
GROUP = PANEL // GROUPS
HALF = GROUP // 2
ORDER = (0, 2, 1, 3)
WAYS = (1, -1, 2)
FIRST = (1, -1, 2)
OFFSETS = (0, -1, 1, -2)
BLOCKS = 64
MESH = pl.DeviceIdType.MESH
F32 = jnp.float32
BF16 = jnp.bfloat16


def rem(value, count):
    return lax.rem(value + count, count)


def kernel(
    density_hbm, reach_hbm, start_hbm, out_ref,
    density_ref, reach_ref, start_ref,
    staged, panel, slab, square_low, extract, extract_in, part, part_in, cube, cube_in, square,
    load_sem, swap_send, swap_recv, ring_send, ring_recv, pair_send, pair_recv, plane_send, plane_recv,
):
    z = lax.axis_index("row")
    col = lax.axis_index("col")
    rep = lax.axis_index("rep")
    x, y_low = lax.div(col, 2), lax.rem(col, 2)
    y_high, core = lax.div(rep, 2), lax.rem(rep, 2)
    y = y_high * 2 + y_low
    other = 1 - core

    def chip_device(x_to, y_to):
        return (z, x_to * 2 + lax.rem(y_to, 2), lax.div(y_to, 2) * 2 + core)

    def chip_index(x_to, y_to):
        return x_to * 4 + lax.rem(y_to, 2) * 2 + lax.div(y_to, 2)

    def step(axis, offset):
        if axis == 0:
            return rem(x + offset, SIDE), y
        return x, rem(y + offset, SIDE)

    def place(first, first_offset, second_offset):
        if first == 0:
            return chip_index(rem(x + first_offset, SIDE), rem(y + second_offset, SIDE))
        return chip_index(rem(x + second_offset, SIDE), rem(y + first_offset, SIDE))

    up = (rem(z + 1, PLANES), col, rep)
    down = (rem(z - 1, PLANES), col, rep)
    sibling = (z, col, y_high * 2 + other)
    chip = chip_index(x, y)

    barrier = pltpu.get_barrier_semaphore()
    partners = [up, down]
    for axis in (0, 1):
        for offset in (1, -1):
            partners.append(chip_device(*step(axis, offset)))
    partners.append(chip_device(*step(0, 2)))
    for offset in (1, 2, 3):
        partners.append((z, col, rem(rep + offset, 4)))
    for partner in partners:
        pl.semaphore_signal(barrier, inc=1, device_id=partner, device_id_type=MESH)

    loads = [
        pltpu.make_async_copy(reach_hbm, reach_ref, load_sem.at[0]),
        pltpu.make_async_copy(density_hbm, density_ref, load_sem.at[1]),
        pltpu.make_async_copy(start_hbm, start_ref, load_sem.at[2]),
    ]
    for load in loads:
        load.start()
    for load in loads:
        load.wait()
    own_block = z * 4 + rep
    own_reach = reach_ref[own_block]
    for block in range(8):
        column_block = col * 8 + block
        spread = lax.abs(column_block - own_block)
        spread = lax.min(spread, BLOCKS - spread)
        kept = spread <= lax.min(reach_ref[column_block], own_reach)
        scale = jnp.where(kept, 1.0, 0.0).astype(F32)
        values = density_ref[:, block * BLOCK:(block + 1) * BLOCK].astype(F32) * scale
        place_at = pl.ds(ORDER[block % 4] * BLOCK, BLOCK)
        staged[block // 4, :, place_at] = values.astype(BF16)
    pl.semaphore_wait(barrier, len(partners))

    def swap_copy(half):
        rows = half * 64
        return pltpu.make_async_remote_copy(
            src_ref=staged.at[1 - y_high, pl.ds(rows, 64)],
            dst_ref=panel.at[z, y_high, pl.ds(rows, 64)],
            send_sem=swap_send.at[half],
            recv_sem=swap_recv.at[half],
            device_id=(z, col, (1 - y_high) * 2 + core),
            device_id_type=MESH,
        )

    for half in (0, 1):
        swap_copy(half).start()
    panel[z, y_high] = staged[y_high]

    def ring_copy(way, distance, quarter):
        behind = distance - 1
        slot = rem(z - behind, PLANES) if way == 0 else rem(z + behind, PLANES)
        where = panel.at[slot, y_high if quarter < 2 else 1 - y_high, pl.ds((quarter % 2) * 64, 64)]
        return pltpu.make_async_remote_copy(
            src_ref=where,
            dst_ref=where,
            send_sem=ring_send,
            recv_sem=ring_recv.at[way, behind, quarter],
            device_id=up if way == 0 else down,
            device_id_type=MESH,
        )

    own = [(way, quarter) for quarter in (0, 1) for way in (0, 1)]
    swapped = [(way, quarter) for quarter in (2, 3) for way in (0, 1)]

    def hand_on(distance, pieces):
        for way, quarter in pieces:
            ring_copy(way, distance - 1, quarter).wait_recv()
            ring_copy(way, distance, quarter).start()

    def arrived(distance, pieces):
        for way, quarter in pieces:
            ring_copy(way, distance, quarter).wait_recv()

    for way, quarter in own:
        ring_copy(way, 1, quarter).start()
    hand_on(2, own)
    for way, quarter in swapped:
        if way == 0:
            swap_copy(quarter - 2).wait_recv()
        ring_copy(way, 1, quarter).start()

    def ring_step(distance, carry):
        hand_on(distance + 1, own)
        hand_on(distance, swapped)
        return carry

    lax.fori_loop(2, 7, ring_step, 0)
    own_up, own_down = [(0, 0), (0, 1)], [(1, 0), (1, 1)]
    swapped_up, swapped_down = [(0, 2), (0, 3)], [(1, 2), (1, 3)]
    hand_on(8, own_up)
    hand_on(7, swapped)
    hand_on(8, swapped_down)
    arrived(7, own_down)
    arrived(7, swapped_up)
    arrived(8, own_up)
    arrived(8, swapped_down)

    first_row = start_ref[0] + z * PANEL
    first_block = lax.div(first_row, BLOCK)
    inside = lax.rem(first_row, BLOCK)
    mine = lax.rem(first_block, 2) == core
    wanted = jnp.where(mine, lax.div(first_block, 2), lax.div(first_block + 1, 2))
    held = lax.min(wanted, 2 * PLANES - 2)
    past = (wanted - held) * BLOCK
    flat = panel.reshape(2 * PLANES, BLOCK, WIDE)
    block = flat[pl.ds(held, 2)].reshape(PANEL, WIDE)

    def pair_copy(index, source, target):
        return pltpu.make_async_remote_copy(
            src_ref=source,
            dst_ref=target,
            send_sem=pair_send.at[index],
            recv_sem=pair_recv.at[index],
            device_id=sibling,
            device_id_type=MESH,
        )

    groups = range(GROUPS)
    extracts = [pair_copy(g, extract.at[other, g], extract_in.at[g]) for g in groups]
    for g in groups:
        rows = lax.broadcasted_iota(jnp.int32, (GROUP, PANEL), 0) + g * GROUP
        columns = lax.broadcasted_iota(jnp.int32, (GROUP, PANEL), 1)
        seen = rows + inside
        middle = jnp.logical_and(seen >= BLOCK, seen < 2 * BLOCK)
        wants = jnp.where(jnp.logical_and(mine, seen < BLOCK), seen, seen - BLOCK) + past
        taken = jnp.logical_and(columns == wants, middle != mine)
        pick = jnp.where(taken, 1.0, 0.0).astype(BF16)
        rows_out = jnp.dot(pick, block, preferred_element_type=F32).astype(BF16)
        extract[0, g] = rows_out[:, :PANEL]
        extract[1, g] = rows_out[:, PANEL:]
        extracts[g].start()

    class Gather:
        def __init__(self, phase, g, buffer):
            self.phase, self.g, self.buffer = phase, g, buffer
            self.count = 0
            self.first, self.second = {}, {}

        def send(self, half, axis, way, mine, theirs, number=None):
            at = pl.ds(self.g * GROUP + half * HALF, HALF)
            if number is None:
                number = self.count
                self.count += 1
            sems = dict(
                send_sem=plane_send.at[self.phase],
                recv_sem=plane_recv.at[self.phase, self.g, number],
                device_id=chip_device(*step(axis, way)), device_id_type=MESH)
            pltpu.make_async_remote_copy(
                src_ref=self.buffer.at[mine, at], dst_ref=self.buffer.at[mine, at], **sems).start()

            def arrives():
                pltpu.make_async_remote_copy(
                    src_ref=self.buffer.at[theirs, at], dst_ref=self.buffer.at[theirs, at], **sems).wait_recv()

            return arrives

        def send_second(self, half, offset):
            onward = 1 if offset in (0, -2) else -1
            for way in (1, -1):
                self.second[half, offset, way] = self.send(
                    half, 1 - half, way, place(half, offset, 0), place(half, offset, -way),
                    None if way == onward else 14)

        def start(self):
            for way in FIRST:
                for half in (0, 1):
                    self.first[half, way] = self.send(
                        half, half, way, place(half, 0, 0), place(half, -way, 0))
            for half in (0, 1):
                self.send_second(half, 0)

        def middle(self):
            for way in WAYS:
                for half in (0, 1):
                    self.first[half, way]()
                    self.send_second(half, -way)

        def forward(self):
            for offset in OFFSETS:
                way = 1 if offset in (0, -2) else -1
                for half in (0, 1):
                    self.second[half, offset, way]()
                    self.send(half, 1 - half, way, place(half, offset, -way), place(half, offset, -2 * way), 15)

        def all_of(self, number):
            pltpu.make_async_remote_copy(
                src_ref=self.buffer.at[pl.ds(0, 2), pl.ds(0, PANEL)],
                dst_ref=self.buffer.at[pl.ds(0, 2), pl.ds(0, PANEL)],
                send_sem=plane_send.at[self.phase],
                recv_sem=plane_recv.at[self.phase, self.g, number],
                device_id=sibling, device_id_type=MESH).wait_recv()

        def near(self):
            self.all_of(14)

        def finish(self):
            self.all_of(15)

    NEAR = [(dx, dy) for dx in (0, 1, -1) for dy in (0, 1, -1)]
    FAR = [(2, dy) for dy in (0, 1, -1, 2)] + [(dx, 2) for dx in (0, 1, -1)]

    def product(buffer, g, target, offsets, first):
        rows = pl.ds(g * GROUP, GROUP)
        value = None
        indices = [place(0, dx, dy) for dx, dy in offsets]
        left = jnp.concatenate([buffer[index, rows, :] for index in indices], axis=1)
        right = jnp.concatenate([panel[index].reshape(PANEL, WIDE) for index in indices], axis=0)
        value = jnp.dot(left, right, preferred_element_type=F32)
        for side in (0, 1):
            half = value[:, side * PANEL:(side + 1) * PANEL]
            target[side, g] = half if first else target[side, g] + half

    def all_sent(array, semaphore):
        pltpu.make_async_remote_copy(
            src_ref=array.at[pl.ds(0, PLANES - 1)],
            dst_ref=array.at[pl.ds(0, PLANES - 1)],
            send_sem=semaphore,
            recv_sem=semaphore,
            device_id=sibling,
            device_id_type=MESH,
        ).wait_send()

    slab_gathers = [Gather(0, g, slab) for g in groups]
    square_gathers = [Gather(1, g, square_low) for g in groups]
    squares = [pair_copy(GROUPS + g, part.at[other, g], part_in.at[g]) for g in groups]
    cubes = [pair_copy(2 * GROUPS + g, cube.at[other, g], cube_in.at[g]) for g in groups]

    def slab_start(g):
        extracts[g].wait_recv()
        slab[chip, g * GROUP:(g + 1) * GROUP, :] = extract[core, g] + extract_in[g]
        slab_gathers[g].start()

    def square_near(g):
        slab_gathers[g].near()
        product(slab, g, part, NEAR, True)

    def square_part(g):
        slab_gathers[g].finish()
        product(slab, g, part, FAR, False)
        squares[g].start()

    def square_start(g):
        squares[g].wait_recv()
        square[g] = part[core, g] + part_in[g]
        square_low[chip, g * GROUP:(g + 1) * GROUP, :] = square[g].astype(BF16)
        square_gathers[g].start()

    def cube_near(g):
        squares[g].wait_send()
        square_gathers[g].near()
        product(square_low, g, part, NEAR, True)

    def cube_part(g):
        square_gathers[g].finish()
        product(square_low, g, part, FAR, False)
        for colour in (0, 1):
            own = jnp.where(core == colour, 3.0, 0.0)
            value = own * square[g] - 2.0 * part[colour, g]
            for side in (0, 1):
                cube[side, g, :, colour * BLOCK:(colour + 1) * BLOCK] = value[:, side * BLOCK:(side + 1) * BLOCK]
        cubes[g].start()

    def result(g):
        cubes[g].wait_recv()
        out_ref[g * GROUP:(g + 1) * GROUP, :] = cube[core, g] + cube_in[g]

    slab_start(0)
    slab_start(1)
    all_sent(panel, ring_send)
    for copy in [swap_copy(0), swap_copy(1)] + extracts:
        copy.wait_send()
    slab_gathers[0].middle()
    slab_gathers[1].middle()
    slab_gathers[0].forward()
    slab_gathers[1].forward()
    square_near(0)
    square_near(1)
    square_part(0)
    square_start(0)
    square_part(1)
    square_start(1)
    all_sent(slab, plane_send.at[0])
    square_gathers[0].middle()
    square_gathers[1].middle()
    square_gathers[0].forward()
    square_gathers[1].forward()
    cube_near(0)
    cube_near(1)
    cube_part(0)
    cube_part(1)
    all_sent(square_low, plane_send.at[1])
    result(0)
    result(1)

    for copy in cubes:
        copy.wait_send()


def local(density, reach, slab_start):
    dma = pltpu.SemaphoreType.DMA
    vmem = pl.BlockSpec(memory_space=pltpu.VMEM)
    hbm = pl.BlockSpec(memory_space=pltpu.HBM)
    return pl.pallas_call(
        kernel,
        out_shape=jax.ShapeDtypeStruct((PANEL, PANEL), F32),
        in_specs=[hbm, hbm, hbm],
        out_specs=vmem,
        scratch_shapes=[
            pltpu.VMEM((BLOCK, 8 * BLOCK), BF16),
            pltpu.SMEM((BLOCKS,), jnp.int32),
            pltpu.SMEM((1,), jnp.int32),
            pltpu.VMEM((2, BLOCK, WIDE), BF16),
            pltpu.VMEM((PLANES, 2, BLOCK, WIDE), BF16),
            pltpu.VMEM((CHIPS, PANEL, PANEL), BF16),
            pltpu.VMEM((CHIPS, PANEL, PANEL), BF16),
            pltpu.VMEM((2, GROUPS, GROUP, PANEL), BF16),
            pltpu.VMEM((GROUPS, GROUP, PANEL), BF16),
            pltpu.VMEM((2, GROUPS, GROUP, PANEL), F32),
            pltpu.VMEM((GROUPS, GROUP, PANEL), F32),
            pltpu.VMEM((2, GROUPS, GROUP, PANEL), F32),
            pltpu.VMEM((GROUPS, GROUP, PANEL), F32),
            pltpu.VMEM((GROUPS, GROUP, PANEL), F32),
            dma((3,)),
            dma((2,)), dma((2,)),
            dma, dma((2, 8, 4)),
            dma((3 * GROUPS,)), dma((3 * GROUPS,)),
            dma((2,)), dma((2, GROUPS, 16)),
        ],
        compiler_params=pltpu.CompilerParams(
            collective_id=0, has_side_effects=True, vmem_limit_bytes=40 * 1024 * 1024),
    )(density, reach, slab_start)


def solution(mesh):
    return jax.shard_map(
        local,
        mesh=mesh,
        in_specs=(P(("row", "rep"), "col"), P(), P()),
        out_specs=P("row", ("col", "rep")),
        check_vma=False,
    )
```

```python
import jax
import jax.numpy as jnp
from jax import lax
from jax.experimental import pallas as pl
from jax.experimental.pallas import tpu as pltpu
from jax.sharding import PartitionSpec as P

BLOCK = 128
PANEL = 256
WIDE = 512
PLANES = 16
CHIPS = 16
SIDE = 4
GROUPS = 2
GROUP = PANEL // GROUPS
HALF = GROUP // 2
ORDER = (0, 2, 1, 3)
WAYS = (1, -1, 2)
FIRST = (1, -1, 2)
OFFSETS = (0, -1, 1, -2)
BLOCKS = 64
MESH = pl.DeviceIdType.MESH
F32 = jnp.float32
BF16 = jnp.bfloat16


def rem(value, count):
    return lax.rem(value + count, count)


def kernel(
    density_hbm, reach_hbm, start_hbm, out_ref,
    density_ref, reach_ref, start_ref,
    staged, panel, slab, square_low, extract, extract_in, part, part_in, cube, cube_in, square,
    load_sem, swap_send, swap_recv, ring_send, ring_recv, pair_send, pair_recv, plane_send, plane_recv,
):
    z = lax.axis_index("row")
    col = lax.axis_index("col")
    rep = lax.axis_index("rep")
    x, y_low = lax.div(col, 2), lax.rem(col, 2)
    y_high, core = lax.div(rep, 2), lax.rem(rep, 2)
    y = y_high * 2 + y_low
    other = 1 - core

    def chip_device(x_to, y_to):
        return (z, x_to * 2 + lax.rem(y_to, 2), lax.div(y_to, 2) * 2 + core)

    def chip_index(x_to, y_to):
        return x_to * 4 + lax.rem(y_to, 2) * 2 + lax.div(y_to, 2)

    def step(axis, offset):
        if axis == 0:
            return rem(x + offset, SIDE), y
        return x, rem(y + offset, SIDE)

    def place(first, first_offset, second_offset):
        if first == 0:
            return chip_index(rem(x + first_offset, SIDE), rem(y + second_offset, SIDE))
        return chip_index(rem(x + second_offset, SIDE), rem(y + first_offset, SIDE))

    up = (rem(z + 1, PLANES), col, rep)
    down = (rem(z - 1, PLANES), col, rep)
    sibling = (z, col, y_high * 2 + other)
    chip = chip_index(x, y)

    barrier = pltpu.get_barrier_semaphore()
    partners = [up, down]
    for axis in (0, 1):
        for offset in (1, -1):
            partners.append(chip_device(*step(axis, offset)))
    partners.append(chip_device(*step(0, 2)))
    for offset in (1, 2, 3):
        partners.append((z, col, rem(rep + offset, 4)))
    for partner in partners:
        pl.semaphore_signal(barrier, inc=1, device_id=partner, device_id_type=MESH)

    loads = [
        pltpu.make_async_copy(reach_hbm, reach_ref, load_sem.at[0]),
        pltpu.make_async_copy(density_hbm, density_ref, load_sem.at[1]),
        pltpu.make_async_copy(start_hbm, start_ref, load_sem.at[2]),
    ]
    for load in loads:
        load.start()
    for load in loads:
        load.wait()
    own_block = z * 4 + rep
    own_reach = reach_ref[own_block]
    for block in range(8):
        column_block = col * 8 + block
        spread = lax.abs(column_block - own_block)
        spread = lax.min(spread, BLOCKS - spread)
        kept = spread <= lax.min(reach_ref[column_block], own_reach)
        scale = jnp.where(kept, 1.0, 0.0).astype(F32)
        values = density_ref[:, block * BLOCK:(block + 1) * BLOCK].astype(F32) * scale
        place_at = pl.ds(ORDER[block % 4] * BLOCK, BLOCK)
        staged[block // 4, :, place_at] = values.astype(BF16)
    pl.semaphore_wait(barrier, len(partners))

    def swap_copy(half):
        rows = half * 64
        return pltpu.make_async_remote_copy(
            src_ref=staged.at[1 - y_high, pl.ds(rows, 64)],
            dst_ref=panel.at[z, y_high, pl.ds(rows, 64)],
            send_sem=swap_send.at[half],
            recv_sem=swap_recv.at[half],
            device_id=(z, col, (1 - y_high) * 2 + core),
            device_id_type=MESH,
        )

    for half in (0, 1):
        swap_copy(half).start()
    panel[z, y_high] = staged[y_high]

    def ring_copy(way, distance, quarter):
        behind = distance - 1
        slot = rem(z - behind, PLANES) if way == 0 else rem(z + behind, PLANES)
        where = panel.at[slot, y_high if quarter < 4 else 1 - y_high, pl.ds((quarter % 4) * 32, 32)]
        return pltpu.make_async_remote_copy(
            src_ref=where,
            dst_ref=where,
            send_sem=ring_send,
            recv_sem=ring_recv.at[way, behind, quarter],
            device_id=up if way == 0 else down,
            device_id_type=MESH,
        )

    own = [(way, quarter) for quarter in range(4) for way in (0, 1)]
    swapped = [(way, quarter) for quarter in range(4, 8) for way in (0, 1)]

    def hand_on(distance, pieces):
        for way, quarter in pieces:
            ring_copy(way, distance - 1, quarter).wait_recv()
            ring_copy(way, distance, quarter).start()

    def arrived(distance, pieces):
        for way, quarter in pieces:
            ring_copy(way, distance, quarter).wait_recv()

    for way, quarter in own:
        ring_copy(way, 1, quarter).start()
    hand_on(2, own)
    for way, quarter in swapped:
        if way == 0 and (quarter - 4) % 2 == 0:
            swap_copy((quarter - 4) // 2).wait_recv()
        ring_copy(way, 1, quarter).start()

    def ring_step(distance, carry):
        hand_on(distance + 1, own)
        hand_on(distance, swapped)
        return carry

    lax.fori_loop(2, 7, ring_step, 0)
    own_up, own_down = own[::2], own[1::2]
    swapped_up, swapped_down = swapped[::2], swapped[1::2]
    hand_on(8, own_up)
    hand_on(7, swapped)
    hand_on(8, swapped_down)
    arrived(7, own_down)
    arrived(7, swapped_up)
    arrived(8, own_up)
    arrived(8, swapped_down)

    first_row = start_ref[0] + z * PANEL
    first_block = lax.div(first_row, BLOCK)
    inside = lax.rem(first_row, BLOCK)
    mine = lax.rem(first_block, 2) == core
    wanted = jnp.where(mine, lax.div(first_block, 2), lax.div(first_block + 1, 2))
    held = lax.min(wanted, 2 * PLANES - 2)
    past = (wanted - held) * BLOCK
    flat = panel.reshape(2 * PLANES, BLOCK, WIDE)
    block = flat[pl.ds(held, 2)].reshape(PANEL, WIDE)

    def pair_copy(index, source, target):
        return pltpu.make_async_remote_copy(
            src_ref=source,
            dst_ref=target,
            send_sem=pair_send.at[index],
            recv_sem=pair_recv.at[index],
            device_id=sibling,
            device_id_type=MESH,
        )

    groups = range(GROUPS)
    extracts = [pair_copy(g, extract.at[other, g], extract_in.at[g]) for g in groups]
    for g in groups:
        rows = lax.broadcasted_iota(jnp.int32, (GROUP, PANEL), 0) + g * GROUP
        columns = lax.broadcasted_iota(jnp.int32, (GROUP, PANEL), 1)
        seen = rows + inside
        middle = jnp.logical_and(seen >= BLOCK, seen < 2 * BLOCK)
        wants = jnp.where(jnp.logical_and(mine, seen < BLOCK), seen, seen - BLOCK) + past
        taken = jnp.logical_and(columns == wants, middle != mine)
        pick = jnp.where(taken, 1.0, 0.0).astype(BF16)
        rows_out = jnp.dot(pick, block, preferred_element_type=F32).astype(BF16)
        extract[0, g] = rows_out[:, :PANEL]
        extract[1, g] = rows_out[:, PANEL:]
        extracts[g].start()

    class Gather:
        def __init__(self, phase, g, buffer):
            self.phase, self.g, self.buffer = phase, g, buffer
            self.count = 0
            self.first, self.second = {}, {}

        def send(self, half, axis, way, mine, theirs, number=None):
            at = pl.ds(self.g * GROUP + half * HALF, HALF)
            if number is None:
                number = self.count
                self.count += 1
            sems = dict(
                send_sem=plane_send.at[self.phase],
                recv_sem=plane_recv.at[self.phase, self.g, number],
                device_id=chip_device(*step(axis, way)), device_id_type=MESH)
            pltpu.make_async_remote_copy(
                src_ref=self.buffer.at[mine, at], dst_ref=self.buffer.at[mine, at], **sems).start()

            def arrives():
                pltpu.make_async_remote_copy(
                    src_ref=self.buffer.at[theirs, at], dst_ref=self.buffer.at[theirs, at], **sems).wait_recv()

            return arrives

        def send_second(self, half, offset):
            onward = 1 if offset in (0, -1) else -1
            for way in (1, -1):
                self.second[half, offset, way] = self.send(
                    half, 1 - half, way, place(half, offset, 0), place(half, offset, -way),
                    None if way == onward else 14)

        def start(self):
            for way in FIRST:
                for half in (0, 1):
                    self.first[half, way] = self.send(
                        half, half, way, place(half, 0, 0), place(half, -way, 0))
            for half in (0, 1):
                self.send_second(half, 0)

        def middle(self):
            for way in WAYS:
                for half in (0, 1):
                    self.first[half, way]()
                    self.send_second(half, -way)

        def forward(self):
            for offset in OFFSETS:
                way = 1 if offset in (0, -1) else -1
                for half in (0, 1):
                    self.second[half, offset, way]()
                    self.send(half, 1 - half, way, place(half, offset, -way), place(half, offset, -2 * way), 15)

        def all_of(self, number):
            pltpu.make_async_remote_copy(
                src_ref=self.buffer.at[pl.ds(0, 2), pl.ds(0, PANEL)],
                dst_ref=self.buffer.at[pl.ds(0, 2), pl.ds(0, PANEL)],
                send_sem=plane_send.at[self.phase],
                recv_sem=plane_recv.at[self.phase, self.g, number],
                device_id=sibling, device_id_type=MESH).wait_recv()

        def near(self):
            self.all_of(14)

        def finish(self):
            self.all_of(15)

    NEAR = [(dx, dy) for dx in (0, 1, -1) for dy in (0, 1, -1)]
    FAR = [(2, dy) for dy in (0, 1, -1, 2)] + [(dx, 2) for dx in (0, 1, -1)]

    def product(buffer, g, target, offsets, first):
        rows = pl.ds(g * GROUP, GROUP)
        value = None
        indices = [place(0, dx, dy) for dx, dy in offsets]
        left = jnp.concatenate([buffer[index, rows, :] for index in indices], axis=1)
        right = jnp.concatenate([panel[index].reshape(PANEL, WIDE) for index in indices], axis=0)
        value = jnp.dot(left, right, preferred_element_type=F32)
        for side in (0, 1):
            half = value[:, side * PANEL:(side + 1) * PANEL]
            target[side, g] = half if first else target[side, g] + half

    def all_sent(array, semaphore):
        pltpu.make_async_remote_copy(
            src_ref=array.at[pl.ds(0, PLANES - 1)],
            dst_ref=array.at[pl.ds(0, PLANES - 1)],
            send_sem=semaphore,
            recv_sem=semaphore,
            device_id=sibling,
            device_id_type=MESH,
        ).wait_send()

    slab_gathers = [Gather(0, g, slab) for g in groups]
    square_gathers = [Gather(1, g, square_low) for g in groups]
    squares = [pair_copy(GROUPS + g, part.at[other, g], part_in.at[g]) for g in groups]
    cubes = [pair_copy(2 * GROUPS + g, cube.at[other, g], cube_in.at[g]) for g in groups]

    def slab_start(g):
        extracts[g].wait_recv()
        slab[chip, g * GROUP:(g + 1) * GROUP, :] = extract[core, g] + extract_in[g]
        slab_gathers[g].start()

    def square_near(g):
        slab_gathers[g].near()
        product(slab, g, part, NEAR, True)

    def square_part(g):
        slab_gathers[g].finish()
        product(slab, g, part, FAR, False)
        squares[g].start()

    def square_start(g):
        squares[g].wait_recv()
        square[g] = part[core, g] + part_in[g]
        square_low[chip, g * GROUP:(g + 1) * GROUP, :] = square[g].astype(BF16)
        square_gathers[g].start()

    def cube_near(g):
        squares[g].wait_send()
        square_gathers[g].near()
        product(square_low, g, part, NEAR, True)

    def cube_part(g):
        square_gathers[g].finish()
        product(square_low, g, part, FAR, False)
        for colour in (0, 1):
            own = jnp.where(core == colour, 3.0, 0.0)
            value = own * square[g] - 2.0 * part[colour, g]
            for side in (0, 1):
                cube[side, g, :, colour * BLOCK:(colour + 1) * BLOCK] = value[:, side * BLOCK:(side + 1) * BLOCK]
        cubes[g].start()

    def result(g):
        cubes[g].wait_recv()
        out_ref[g * GROUP:(g + 1) * GROUP, :] = cube[core, g] + cube_in[g]

    slab_start(0)
    slab_start(1)
    all_sent(panel, ring_send)
    for copy in [swap_copy(0), swap_copy(1)] + extracts:
        copy.wait_send()
    slab_gathers[0].middle()
    slab_gathers[1].middle()
    slab_gathers[0].forward()
    slab_gathers[1].forward()
    square_near(0)
    square_near(1)
    square_part(0)
    square_start(0)
    square_part(1)
    square_start(1)
    all_sent(slab, plane_send.at[0])
    square_gathers[0].middle()
    square_gathers[1].middle()
    square_gathers[0].forward()
    square_gathers[1].forward()
    cube_near(0)
    cube_near(1)
    cube_part(0)
    result(0)
    cube_part(1)
    all_sent(square_low, plane_send.at[1])
    result(1)

    for copy in cubes:
        copy.wait_send()


def local(density, reach, slab_start):
    dma = pltpu.SemaphoreType.DMA
    vmem = pl.BlockSpec(memory_space=pltpu.VMEM)
    hbm = pl.BlockSpec(memory_space=pltpu.HBM)
    return pl.pallas_call(
        kernel,
        out_shape=jax.ShapeDtypeStruct((PANEL, PANEL), F32),
        in_specs=[hbm, hbm, hbm],
        out_specs=vmem,
        scratch_shapes=[
            pltpu.VMEM((BLOCK, 8 * BLOCK), BF16),
            pltpu.SMEM((BLOCKS,), jnp.int32),
            pltpu.SMEM((1,), jnp.int32),
            pltpu.VMEM((2, BLOCK, WIDE), BF16),
            pltpu.VMEM((PLANES, 2, BLOCK, WIDE), BF16),
            pltpu.VMEM((CHIPS, PANEL, PANEL), BF16),
            pltpu.VMEM((CHIPS, PANEL, PANEL), BF16),
            pltpu.VMEM((2, GROUPS, GROUP, PANEL), BF16),
            pltpu.VMEM((GROUPS, GROUP, PANEL), BF16),
            pltpu.VMEM((2, GROUPS, GROUP, PANEL), F32),
            pltpu.VMEM((GROUPS, GROUP, PANEL), F32),
            pltpu.VMEM((2, GROUPS, GROUP, PANEL), F32),
            pltpu.VMEM((GROUPS, GROUP, PANEL), F32),
            pltpu.VMEM((GROUPS, GROUP, PANEL), F32),
            dma((3,)),
            dma((2,)), dma((2,)),
            dma, dma((2, 8, 8)),
            dma((3 * GROUPS,)), dma((3 * GROUPS,)),
            dma((2,)), dma((2, GROUPS, 16)),
        ],
        compiler_params=pltpu.CompilerParams(
            collective_id=0, has_side_effects=True, vmem_limit_bytes=40 * 1024 * 1024),
    )(density, reach, slab_start)


def solution(mesh):
    return jax.shard_map(
        local,
        mesh=mesh,
        in_specs=(P(("row", "rep"), "col"), P(), P()),
        out_specs=P("row", ("col", "rep")),
        check_vma=False,
    )
```

```python
import jax
import jax.numpy as jnp
from jax import lax
from jax.experimental import pallas as pl
from jax.experimental.pallas import tpu as pltpu
from jax.sharding import PartitionSpec as P

BLOCK = 128
PANEL = 256
WIDE = 512
PLANES = 16
CHIPS = 16
SIDE = 4
GROUPS = 2
GROUP = PANEL // GROUPS
HALF = GROUP // 2
ORDER = (0, 2, 1, 3)
WAYS = (1, -1, 2)
FIRST = (1, -1, 2)
OFFSETS = (0, -1, 1, -2)
BLOCKS = 64
MESH = pl.DeviceIdType.MESH
F32 = jnp.float32
BF16 = jnp.bfloat16


def rem(value, count):
    return lax.rem(value + count, count)


def kernel(
    density_ref, reach_hbm, start_hbm, out_ref,
    reach_ref, start_ref,
    staged, panel, slab, square_low, extract, extract_in, part, part_in, cube, cube_in, square,
    load_sem, swap_send, swap_recv, ring_send, ring_recv, pair_send, pair_recv, plane_send, plane_recv,
):
    z = lax.axis_index("row")
    col = lax.axis_index("col")
    rep = lax.axis_index("rep")
    x, y_low = lax.div(col, 2), lax.rem(col, 2)
    y_high, core = lax.div(rep, 2), lax.rem(rep, 2)
    y = y_high * 2 + y_low
    other = 1 - core

    def chip_device(x_to, y_to):
        return (z, x_to * 2 + lax.rem(y_to, 2), lax.div(y_to, 2) * 2 + core)

    def chip_index(x_to, y_to):
        return x_to * 4 + lax.rem(y_to, 2) * 2 + lax.div(y_to, 2)

    def step(axis, offset):
        if axis == 0:
            return rem(x + offset, SIDE), y
        return x, rem(y + offset, SIDE)

    def place(first, first_offset, second_offset):
        if first == 0:
            return chip_index(rem(x + first_offset, SIDE), rem(y + second_offset, SIDE))
        return chip_index(rem(x + second_offset, SIDE), rem(y + first_offset, SIDE))

    up = (rem(z + 1, PLANES), col, rep)
    down = (rem(z - 1, PLANES), col, rep)
    sibling = (z, col, y_high * 2 + other)
    chip = chip_index(x, y)

    barrier = pltpu.get_barrier_semaphore()
    partners = [up, down]
    for axis in (0, 1):
        for offset in (1, -1):
            partners.append(chip_device(*step(axis, offset)))
    partners.append(chip_device(*step(0, 2)))
    for offset in (1, 2, 3):
        partners.append((z, col, rem(rep + offset, 4)))
    for partner in partners:
        pl.semaphore_signal(barrier, inc=1, device_id=partner, device_id_type=MESH)

    loads = [
        pltpu.make_async_copy(reach_hbm, reach_ref, load_sem.at[0]),
        pltpu.make_async_copy(start_hbm, start_ref, load_sem.at[2]),
    ]
    for load in loads:
        load.start()
    for load in loads:
        load.wait()
    own_block = z * 4 + rep
    own_reach = reach_ref[own_block]
    for block in range(8):
        column_block = col * 8 + block
        spread = lax.abs(column_block - own_block)
        spread = lax.min(spread, BLOCKS - spread)
        kept = spread <= lax.min(reach_ref[column_block], own_reach)
        scale = jnp.where(kept, 1.0, 0.0).astype(F32)
        values = density_ref[:, block * BLOCK:(block + 1) * BLOCK].astype(F32) * scale
        place_at = pl.ds(ORDER[block % 4] * BLOCK, BLOCK)
        staged[block // 4, :, place_at] = values.astype(BF16)
    pl.semaphore_wait(barrier, len(partners))

    def swap_copy(half):
        rows = half * 64
        return pltpu.make_async_remote_copy(
            src_ref=staged.at[1 - y_high, pl.ds(rows, 64)],
            dst_ref=panel.at[z, y_high, pl.ds(rows, 64)],
            send_sem=swap_send.at[half],
            recv_sem=swap_recv.at[half],
            device_id=(z, col, (1 - y_high) * 2 + core),
            device_id_type=MESH,
        )

    for half in (0, 1):
        swap_copy(half).start()
    panel[z, y_high] = staged[y_high]

    def ring_copy(way, distance, quarter):
        behind = distance - 1
        slot = rem(z - behind, PLANES) if way == 0 else rem(z + behind, PLANES)
        where = panel.at[slot, y_high if quarter < 4 else 1 - y_high, pl.ds((quarter % 4) * 32, 32)]
        return pltpu.make_async_remote_copy(
            src_ref=where,
            dst_ref=where,
            send_sem=ring_send,
            recv_sem=ring_recv.at[way, behind, quarter],
            device_id=up if way == 0 else down,
            device_id_type=MESH,
        )

    own = [(way, quarter) for quarter in range(4) for way in (0, 1)]
    swapped = [(way, quarter) for quarter in range(4, 8) for way in (0, 1)]

    def hand_on(distance, pieces):
        for way, quarter in pieces:
            ring_copy(way, distance - 1, quarter).wait_recv()
            ring_copy(way, distance, quarter).start()

    def arrived(distance, pieces):
        for way, quarter in pieces:
            ring_copy(way, distance, quarter).wait_recv()

    for way, quarter in own:
        ring_copy(way, 1, quarter).start()
    hand_on(2, own)
    for way, quarter in swapped:
        if way == 0 and (quarter - 4) % 2 == 0:
            swap_copy((quarter - 4) // 2).wait_recv()
        ring_copy(way, 1, quarter).start()

    def ring_step(distance, carry):
        hand_on(distance + 1, own)
        hand_on(distance, swapped)
        return carry

    lax.fori_loop(2, 7, ring_step, 0)
    own_up, own_down = own[::2], own[1::2]
    swapped_up, swapped_down = swapped[::2], swapped[1::2]
    hand_on(8, own_up)
    hand_on(7, swapped)
    hand_on(8, swapped_down)
    arrived(7, own_down)
    arrived(7, swapped_up)
    arrived(8, own_up)
    arrived(8, swapped_down)

    first_row = start_ref[0] + z * PANEL
    first_block = lax.div(first_row, BLOCK)
    inside = lax.rem(first_row, BLOCK)
    mine = lax.rem(first_block, 2) == core
    wanted = jnp.where(mine, lax.div(first_block, 2), lax.div(first_block + 1, 2))
    held = lax.min(wanted, 2 * PLANES - 2)
    past = (wanted - held) * BLOCK
    flat = panel.reshape(2 * PLANES, BLOCK, WIDE)
    block = flat[pl.ds(held, 2)].reshape(PANEL, WIDE)

    def pair_copy(index, source, target):
        return pltpu.make_async_remote_copy(
            src_ref=source,
            dst_ref=target,
            send_sem=pair_send.at[index],
            recv_sem=pair_recv.at[index],
            device_id=sibling,
            device_id_type=MESH,
        )

    groups = range(GROUPS)
    extracts = [pair_copy(g, extract.at[other, g], extract_in.at[g]) for g in groups]
    for g in groups:
        rows = lax.broadcasted_iota(jnp.int32, (GROUP, PANEL), 0) + g * GROUP
        columns = lax.broadcasted_iota(jnp.int32, (GROUP, PANEL), 1)
        seen = rows + inside
        middle = jnp.logical_and(seen >= BLOCK, seen < 2 * BLOCK)
        wants = jnp.where(jnp.logical_and(mine, seen < BLOCK), seen, seen - BLOCK) + past
        taken = jnp.logical_and(columns == wants, middle != mine)
        pick = jnp.where(taken, 1.0, 0.0).astype(BF16)
        rows_out = jnp.dot(pick, block, preferred_element_type=F32).astype(BF16)
        extract[0, g] = rows_out[:, :PANEL]
        extract[1, g] = rows_out[:, PANEL:]
        extracts[g].start()

    class Gather:
        def __init__(self, phase, g, buffer):
            self.phase, self.g, self.buffer = phase, g, buffer
            self.count = 0
            self.first, self.second = {}, {}

        def send(self, half, axis, way, mine, theirs, number=None):
            at = pl.ds(self.g * GROUP + half * HALF, HALF)
            if number is None:
                number = self.count
                self.count += 1
            sems = dict(
                send_sem=plane_send.at[self.phase],
                recv_sem=plane_recv.at[self.phase, self.g, number],
                device_id=chip_device(*step(axis, way)), device_id_type=MESH)
            pltpu.make_async_remote_copy(
                src_ref=self.buffer.at[mine, at], dst_ref=self.buffer.at[mine, at], **sems).start()

            def arrives():
                pltpu.make_async_remote_copy(
                    src_ref=self.buffer.at[theirs, at], dst_ref=self.buffer.at[theirs, at], **sems).wait_recv()

            return arrives

        def send_second(self, half, offset):
            onward = 1 if offset in (0, -1) else -1
            for way in (1, -1):
                self.second[half, offset, way] = self.send(
                    half, 1 - half, way, place(half, offset, 0), place(half, offset, -way),
                    None if way == onward else 14)

        def start(self):
            for way in FIRST:
                for half in (0, 1):
                    self.first[half, way] = self.send(
                        half, half, way, place(half, 0, 0), place(half, -way, 0))
            for half in (0, 1):
                self.send_second(half, 0)

        def middle(self):
            for way in WAYS:
                for half in (0, 1):
                    self.first[half, way]()
                    self.send_second(half, -way)

        def forward(self):
            for offset in OFFSETS:
                way = 1 if offset in (0, -1) else -1
                for half in (0, 1):
                    self.second[half, offset, way]()
                    self.send(half, 1 - half, way, place(half, offset, -way), place(half, offset, -2 * way), 15)

        def all_of(self, number):
            pltpu.make_async_remote_copy(
                src_ref=self.buffer.at[pl.ds(0, 2), pl.ds(0, PANEL)],
                dst_ref=self.buffer.at[pl.ds(0, 2), pl.ds(0, PANEL)],
                send_sem=plane_send.at[self.phase],
                recv_sem=plane_recv.at[self.phase, self.g, number],
                device_id=sibling, device_id_type=MESH).wait_recv()

        def near(self):
            self.all_of(14)

        def finish(self):
            self.all_of(15)

    NEAR = [(dx, dy) for dx in (0, 1, -1) for dy in (0, 1, -1)]
    FAR = [(2, dy) for dy in (0, 1, -1, 2)] + [(dx, 2) for dx in (0, 1, -1)]

    def product(buffer, g, target, offsets, first):
        rows = pl.ds(g * GROUP, GROUP)
        value = None
        indices = [place(0, dx, dy) for dx, dy in offsets]
        left = jnp.concatenate([buffer[index, rows, :] for index in indices], axis=1)
        right = jnp.concatenate([panel[index].reshape(PANEL, WIDE) for index in indices], axis=0)
        value = jnp.dot(left, right, preferred_element_type=F32)
        for side in (0, 1):
            half = value[:, side * PANEL:(side + 1) * PANEL]
            target[side, g] = half if first else target[side, g] + half

    def all_sent(array, semaphore):
        pltpu.make_async_remote_copy(
            src_ref=array.at[pl.ds(0, PLANES - 1)],
            dst_ref=array.at[pl.ds(0, PLANES - 1)],
            send_sem=semaphore,
            recv_sem=semaphore,
            device_id=sibling,
            device_id_type=MESH,
        ).wait_send()

    slab_gathers = [Gather(0, g, slab) for g in groups]
    square_gathers = [Gather(1, g, square_low) for g in groups]
    squares = [pair_copy(GROUPS + g, part.at[other, g], part_in.at[g]) for g in groups]
    cubes = [pair_copy(2 * GROUPS + g, cube.at[other, g], cube_in.at[g]) for g in groups]

    def slab_start(g):
        extracts[g].wait_recv()
        slab[chip, g * GROUP:(g + 1) * GROUP, :] = extract[core, g] + extract_in[g]
        slab_gathers[g].start()

    def square_near(g):
        slab_gathers[g].near()
        product(slab, g, part, NEAR, True)

    def square_part(g):
        slab_gathers[g].finish()
        product(slab, g, part, FAR, False)
        squares[g].start()

    def square_start(g):
        squares[g].wait_recv()
        square[g] = part[core, g] + part_in[g]
        square_low[chip, g * GROUP:(g + 1) * GROUP, :] = square[g].astype(BF16)
        square_gathers[g].start()

    def cube_near(g):
        squares[g].wait_send()
        square_gathers[g].near()
        product(square_low, g, part, NEAR, True)

    def cube_part(g):
        square_gathers[g].finish()
        product(square_low, g, part, FAR, False)
        for colour in (0, 1):
            own = jnp.where(core == colour, 3.0, 0.0)
            value = own * square[g] - 2.0 * part[colour, g]
            for side in (0, 1):
                cube[side, g, :, colour * BLOCK:(colour + 1) * BLOCK] = value[:, side * BLOCK:(side + 1) * BLOCK]
        cubes[g].start()

    def result(g):
        cubes[g].wait_recv()
        out_ref[g * GROUP:(g + 1) * GROUP, :] = cube[core, g] + cube_in[g]

    slab_start(0)
    slab_start(1)
    all_sent(panel, ring_send)
    for copy in [swap_copy(0), swap_copy(1)] + extracts:
        copy.wait_send()
    slab_gathers[0].middle()
    slab_gathers[1].middle()
    slab_gathers[0].forward()
    slab_gathers[1].forward()
    square_near(0)
    square_near(1)
    square_part(0)
    square_start(0)
    square_part(1)
    square_start(1)
    all_sent(slab, plane_send.at[0])
    square_gathers[0].middle()
    square_gathers[1].middle()
    square_gathers[0].forward()
    square_gathers[1].forward()
    cube_near(0)
    cube_near(1)
    cube_part(0)
    result(0)
    cube_part(1)
    all_sent(square_low, plane_send.at[1])
    result(1)

    for copy in cubes:
        copy.wait_send()


def local(density, reach, slab_start):
    dma = pltpu.SemaphoreType.DMA
    vmem = pl.BlockSpec(memory_space=pltpu.VMEM)
    hbm = pl.BlockSpec(memory_space=pltpu.HBM)
    return pl.pallas_call(
        kernel,
        out_shape=jax.ShapeDtypeStruct((PANEL, PANEL), F32),
        in_specs=[vmem, hbm, hbm],
        out_specs=vmem,
        scratch_shapes=[
            pltpu.SMEM((BLOCKS,), jnp.int32),
            pltpu.SMEM((1,), jnp.int32),
            pltpu.VMEM((2, BLOCK, WIDE), BF16),
            pltpu.VMEM((PLANES, 2, BLOCK, WIDE), BF16),
            pltpu.VMEM((CHIPS, PANEL, PANEL), BF16),
            pltpu.VMEM((CHIPS, PANEL, PANEL), BF16),
            pltpu.VMEM((2, GROUPS, GROUP, PANEL), BF16),
            pltpu.VMEM((GROUPS, GROUP, PANEL), BF16),
            pltpu.VMEM((2, GROUPS, GROUP, PANEL), F32),
            pltpu.VMEM((GROUPS, GROUP, PANEL), F32),
            pltpu.VMEM((2, GROUPS, GROUP, PANEL), F32),
            pltpu.VMEM((GROUPS, GROUP, PANEL), F32),
            pltpu.VMEM((GROUPS, GROUP, PANEL), F32),
            dma((3,)),
            dma((2,)), dma((2,)),
            dma, dma((2, 8, 8)),
            dma((3 * GROUPS,)), dma((3 * GROUPS,)),
            dma((2,)), dma((2, GROUPS, 16)),
        ],
        compiler_params=pltpu.CompilerParams(
            collective_id=0, has_side_effects=True, vmem_limit_bytes=40 * 1024 * 1024),
    )(density, reach, slab_start)


def solution(mesh):
    return jax.shard_map(
        local,
        mesh=mesh,
        in_specs=(P(("row", "rep"), "col"), P(), P()),
        out_specs=P("row", ("col", "rep")),
        check_vma=False,
    )
```
